256 devices in a mesh: stretch: 32 (over z, x), rows: 2 (over core), cols: 4 (over y).
Axes of the slice: x: 4, y: 4, z: 8, core: 2. Of those that a mesh axis runs over, the one named last changes fastest.
Arguments:
- latent: bfloat16 [128, 16, 1536], P('stretch', 'rows', 'cols'), may hold values from -6 to 6
- frame_counts: int32 [32], replicated, may hold values from 1 to 4, 97 in all
- row_counts: int32 [2], replicated, may hold values from 1 to 8, 12 in all
- w_in: bfloat16 [3, 3, 3, 16, 384], replicated, may hold values from -0.3125 to 0.3125
- b_in: float32 [384], replicated, may hold values from -3 to 3
- gain_one: float32 [384], replicated, may hold values from 0.1 to 1.9
- w_one: bfloat16 [3, 3, 3, 384, 384], replicated, may hold values from -0.0625 to 0.0625
- b_one: float32 [384], replicated, may hold values from -3 to 3
- gain_two: float32 [384], replicated, may hold values from 0.1 to 1.9
- w_two: bfloat16 [3, 3, 3, 384, 384], replicated, may hold values from -0.0625 to 0.0625
- b_two: float32 [384], replicated, may hold values from -3 to 3
Outputs:
- decoded: bfloat16 [128, 16, 96, 384], P('stretch', 'rows', 'cols')
The draws below stay inside these ranges and needn't reach their ends.
Inputs may be any that keep to these rules, and one draw needn't show every extreme that they name: `frame_counts`: frames in use of each index of stretch; they sum to 97, and some index holds exactly 4. `row_counts`: height rows in use of each index of rows; they sum to 12.
All inputs are finite; a program needn't handle non-finite values.
Results may differ from the reference program's by a relative error of at most 0.014.
Values may be sent and summed in bfloat16 or wider, within the bound.
No kernel may reach another device: no remote copies, remote signals or barrier semaphores. Data moves between devices by JAX's collectives and lax.ppermute only.
A program may use at most 128 MiB of HBM per device.

```python
import math
import jax
import jax.numpy as jnp
import numpy as np
from jax import lax

C = 384
C_IN = 16
F_MAX = 4
R_MAX = 8
FRAMES = 97
HEIGHT = 12
FRAME_SLOTS = 128
ROW_SLOTS = 16
WIDTH = 96
N_STRETCH = 32
N_ROWS = 2


def level_of(stream_key, extent, split, least, high):
    def one(position, blocks):
        draws = jax.random.uniform(jax.random.fold_in(jax.random.fold_in(stream_key, 6), position), (blocks,), jnp.float32, least / len(split), high / len(split))
        return jnp.repeat(jnp.exp(draws), extent[position] // blocks).reshape((-1,) + (1,) * (len(extent) - position - 1))

    loudness = one(*split[0])
    for cut in split[1:]:
        loudness = loudness * one(*cut)
    return loudness


def length_profile(amount, total, most, lean):
    weights = [(1 << 20) // math.isqrt(standing ** lean) + 1 for standing in range(2, amount + 1)]
    spare, given = total - most - (amount - 1), [1] * (amount - 1)
    while spare > 0:
        movable = [i for i in range(amount - 1) if given[i] < most]
        pool, remaining = sum([weights[i] for i in movable]), spare
        for i in movable:
            addition = min(most - given[i], max(1, remaining * weights[i] // pool), spare)
            given[i] = given[i] + addition
            spare = spare - addition
    return np.array([most] + given)


def ragged_sizes(key, number_of, total, reach, lean):
    if number_of == 2:
        one = jax.random.randint(key, (), max(1, total - reach), min(reach, total - 1) + 1)
        return jnp.stack([one, total - one])
    tallies = jnp.asarray(length_profile(number_of, total, reach, lean), jnp.int32)
    twos = (number_of - 1) // 2
    donor, receiver = tallies[1:1 + 2 * twos:2], tallies[2:2 + 2 * twos:2]
    margin = jnp.minimum(donor - 1, reach - receiver)
    shifted = jax.random.randint(jax.random.fold_in(key, 1), (twos,), 0, 1 << 20) % (margin + 1)
    tallies = tallies.at[1:1 + 2 * twos:2].set(donor - shifted).at[2:2 + 2 * twos:2].set(receiver + shifted)
    return tallies[jax.random.permutation(jax.random.fold_in(key, 2), number_of)]


def normal_values(rng, shape, deviation, limit, split=(), kind=jnp.bfloat16):
    array = deviation * jax.random.normal(rng, shape, jnp.float32)
    if split:
        array = array * level_of(rng, shape, split, -0.22, 0.18)
    return jnp.clip(array, -limit, limit).astype(kind)


def setup_inputs(seed: int = 0) -> dict:
    arg_keys = jax.random.split(jax.random.key(seed), 12)
    return {
        "latent": normal_values(arg_keys[0], (FRAME_SLOTS, ROW_SLOTS, WIDTH * C_IN), 1.0, 6.0, ((0, 32), (1, 2), (2, 4))),
        "frame_counts": ragged_sizes(arg_keys[1], N_STRETCH, FRAMES, F_MAX, 1).astype(jnp.int32),
        "row_counts": ragged_sizes(arg_keys[2], N_ROWS, HEIGHT, R_MAX, 1).astype(jnp.int32),
        "w_in": normal_values(arg_keys[3], (3, 3, 3, C_IN, C), (27 * C_IN) ** -0.5, 0.3125),
        "b_in": normal_values(arg_keys[4], (C,), 0.5, 3.0, (), jnp.float32),
        "gain_one": jnp.clip(1.0 + 0.18 * jax.random.normal(arg_keys[5], (C,), jnp.float32), 0.1, 1.9),
        "w_one": normal_values(arg_keys[6], (3, 3, 3, C, C), (27 * C) ** -0.5, 0.0625),
        "b_one": normal_values(arg_keys[7], (C,), 0.5, 3.0, (), jnp.float32),
        "gain_two": jnp.clip(1.0 + 0.18 * jax.random.normal(arg_keys[8], (C,), jnp.float32), 0.1, 1.9),
        "w_two": normal_values(arg_keys[9], (3, 3, 3, C, C), (27 * C) ** -0.5, 0.0625),
        "b_two": normal_values(arg_keys[10], (C,), 0.5, 3.0, (), jnp.float32),
    }


def slot_index(counts, most, total):
    ends = jnp.cumsum(counts).astype(jnp.int32)
    place = jnp.arange(total, dtype=jnp.int32)
    owner = lax.optimization_barrier(jnp.sum((ends[None, :] <= place[:, None]).astype(jnp.int32), axis=1)).astype(jnp.int32)
    starts = (ends - counts).astype(jnp.int32)
    return (owner * most + place - starts[owner]).astype(jnp.int32)

def causal_conv(field, weight, bias):
    data = field.astype(jnp.float32)[None]
    padded = jnp.pad(data, ((0, 0), (2, 0), (1, 1), (1, 1), (0, 0)))
    result = lax.conv_general_dilated(padded, weight.astype(jnp.float32), (1, 1, 1), 'VALID', dimension_numbers=('NDHWC', 'DHWIO', 'NDHWC'), precision=lax.Precision.HIGHEST)
    return result[0] + bias

def rms_silu(field, gain):
    values = field.astype(jnp.float32)
    scaled = values * lax.rsqrt(lax.optimization_barrier(jnp.mean(values * values, axis=-1, keepdims=True)) + 1e-06) * gain
    return jax.nn.silu(scaled).astype(jnp.bfloat16)

def reference(latent, frame_counts, row_counts, w_in, b_in, gain_one, w_one, b_one, gain_two, w_two, b_two):
    frame_slot = slot_index(frame_counts, F_MAX, FRAMES)
    row_slot = slot_index(row_counts, R_MAX, HEIGHT)
    grid = latent.reshape(FRAME_SLOTS, ROW_SLOTS, WIDTH, C_IN)
    compact = grid[frame_slot][:, row_slot]
    first = causal_conv(compact, w_in, b_in).astype(jnp.bfloat16)
    act_one = rms_silu(first, gain_one)
    middle = causal_conv(act_one, w_one, b_one).astype(jnp.bfloat16)
    act_two = rms_silu(middle, gain_two)
    final = (first.astype(jnp.float32) + causal_conv(act_two, w_two, b_two)).astype(jnp.bfloat16)
    decoded = jnp.zeros((FRAME_SLOTS, ROW_SLOTS, WIDTH, C), jnp.bfloat16)
    return decoded.at[frame_slot[:, None], row_slot[None, :]].set(final)
```

```python
import functools

import jax
import jax.numpy as jnp
from jax import lax
from jax.experimental import pallas as pl
from jax.experimental.pallas import tpu as pltpu
from jax.sharding import PartitionSpec as P

F32 = jnp.float32
BF16 = jnp.bfloat16
COLS = 32
SLOT = (0, 1, 3)


def rms_silu(values, half_gain):
    inverse = lax.rsqrt(jnp.mean(values * values, axis=-1, keepdims=True) + 1e-06)
    half = values * inverse * half_gain
    return half + half * jnp.tanh(half)


def weight_copies(source, target, sems):
    copies = []
    for dt in range(3):
        for dh in range(3):
            for dw in range(3):
                copies.append(
                    pltpu.make_async_copy(
                        source.at[dt, dh, dw],
                        target.at[SLOT[dt], pl.ds(dh * 384, 384), pl.ds(dw * 384, 384)],
                        sems.at[dt * 9 + dh * 3 + dw],
                    )
                )
    return copies


def transform_weight(weight):
    step = 64

    def one(i, _):
        rows = pl.ds(pl.multiple_of(i * step, step), step)
        ends = weight[0, rows].astype(F32) + weight[3, rows].astype(F32)
        middle = weight[1, rows].astype(F32)
        weight[1, rows] = (ends + middle).astype(BF16)
        weight[2, rows] = (ends - middle).astype(BF16)
        return 0

    lax.fori_loop(0, weight.shape[1] // step, one, 0)


def store_transformed(target, rows, even, odd, pairs):
    here, after = (slice(0, pairs), slice(1, pairs + 1))
    target[0, rows] = (even[:, here] - even[:, after]).astype(BF16)
    target[1, rows] = (0.5 * (odd[:, here] + even[:, after])).astype(BF16)
    target[2, rows] = (0.5 * (even[:, after] - odd[:, here])).astype(BF16)
    target[3, rows] = (odd[:, here] - odd[:, after]).astype(BF16)


def time_conv(field, weight, start, rows):
    pairs = field.shape[2]
    size = rows * pairs * COLS

    def part(q):
        taps = [
            field[q, pl.ds(start + d, rows)].reshape(size, 384) for d in range(3)
        ]
        return jnp.dot(
            jnp.concatenate(taps, -1), weight[q], preferred_element_type=F32
        )

    def joined(wide):
        return (
            wide[:, :384]
            + pltpu.roll(wide[:, 384:768], size - 1, 0)
            + pltpu.roll(wide[:, 768:], size - 2, 0)
        )

    one, two = part(1), part(2)
    even = joined(part(0) + (one + two))
    odd = joined((one - two) - part(3))
    shape = (rows, pairs, COLS, 384)
    return even.reshape(shape), odd.reshape(shape)


def kernel(
    info, x6, w_in, vec, w1_hbm, w2_hbm, out, w1, w2, v1, v2, first_s, sems, *, width, span
):
    used_rows, band, column, start, used_frames = (info[i] for i in range(5))
    copies1 = weight_copies(w1_hbm, w1, sems.at[0])
    copies2 = weight_copies(w2_hbm, w2, sems.at[1])
    for copy in copies1 + copies2:
        copy.start()
    b_in, half_one, b_one, half_two, b_two = (vec[i : i + 1] for i in range(5))
    base_col = column * span

    def inside(shape, axis, shift):
        spot = lax.broadcasted_iota(jnp.int32, shape, axis) + base_col - shift
        return jnp.logical_and(spot >= 0, spot < width)

    zero_row1 = jnp.where(band == 0, 0, used_rows + 2)
    zero_row2 = jnp.where(band == 0, 0, used_rows + 1)
    v1[:, pl.ds(zero_row1, 1)] = jnp.zeros((4, 1, 3, COLS, 384), BF16)

    def in_row(j, _):
        b = j + 2 - 2 * band
        parts = []
        for dt in range(3):
            for dh in (0, 2):
                parts.append(x6[dt : dt + 8, b + dh].reshape(8 * COLS, 128))
        first = jnp.dot(jnp.concatenate(parts, -1), w_in[...], preferred_element_type=F32)
        first = (first + b_in).astype(BF16)
        split = first.reshape(4, 2, COLS, 384)
        for e in range(2):
            first_s[e, j] = split[2:, e]
        act = rms_silu(first.astype(F32), half_one).reshape(8, COLS, 384)
        frame = lax.broadcasted_iota(jnp.int32, (8, COLS, 1), 0) + start - 4
        live = jnp.logical_and(inside((8, COLS, 1), 1, 2), frame >= 0)
        act = jnp.where(live, act, 0.0).reshape(1, 4, 2, COLS, 384)
        store_transformed(v1, pl.ds(j + 1 - band, 1), act[:, :, 0], act[:, :, 1], 3)
        return 0

    lax.fori_loop(0, used_rows + 2, in_row, 0)

    for copy in copies1:
        copy.wait()
    transform_weight(w1)

    def mid_rows(g, _):
        i = g * 3
        even, odd = time_conv(v1, w1, i, 3)
        shape = (3, 3, COLS, 1)
        row = lax.broadcasted_iota(jnp.int32, shape, 0) + i
        frame = 2 * lax.broadcasted_iota(jnp.int32, shape, 1) + start - 2
        live = jnp.logical_and(inside(shape, 2, 1), row <= used_rows)
        acts = []
        for e, y in enumerate((even, odd)):
            act = rms_silu(y + b_one, half_two)
            acts.append(jnp.where(jnp.logical_and(live, frame + e >= 0), act, 0.0))
        store_transformed(v2, pl.ds(i + 1 - band, 3), acts[0], acts[1], 2)
        return 0

    lax.fori_loop(0, (used_rows + 3) // 3, mid_rows, 0)
    v2[:, pl.ds(zero_row2, 1)] = jnp.zeros((4, 1, 2, COLS, 384), BF16)

    for copy in copies2:
        copy.wait()
    transform_weight(w2)

    def out_rows(g, _):
        o = g * 4

        @pl.when(o < used_rows)
        def _():
            parts = time_conv(v2, w2, o, 4)
            row = lax.broadcasted_iota(jnp.int32, (4, COLS, 1), 0) + o
            for e in range(2):
                first = first_s[e, pl.ds(o + 2 * band, 4)].astype(F32)
                first = pltpu.roll(first.reshape(8 * COLS, 384), 8 * COLS - 2, 0)
                total = parts[e] + b_two + first.reshape(4, 2, COLS, 384)
                for p in range(2):
                    live = jnp.logical_and(row < used_rows, 2 * p + e < used_frames)
                    value = jnp.where(live, total[:, p], 0.0).astype(BF16)
                    out[2 * p + e, pl.ds(o, 4)] = value[:, :span]

        @pl.when(o >= used_rows)
        def _():
            out[:, pl.ds(o, 4)] = jnp.zeros((4, 4, span, 384), BF16)

        return 0

    lax.fori_loop(0, 2, out_rows, 0)


def shifted(value, steps):
    count = lax.axis_size("stretch")
    return lax.ppermute(value, "stretch", [(i, i + steps) for i in range(count - steps)])


def on_device(
    latent, frame_counts, row_counts, w_in, b_in, gain_one, w_one, b_one, gain_two, w_two, b_two
):
    depth, slots, packed = latent.shape
    inner = w_in.shape[3]
    span = packed // inner
    halo = 3
    group = lax.axis_index("stretch")
    band = lax.axis_index("rows")
    column = lax.axis_index("cols")
    n_cols = lax.axis_size("cols")
    n_groups = lax.axis_size("stretch")
    used_rows = row_counts[band]
    used_frames = frame_counts[group]
    ends = jnp.cumsum(frame_counts)
    start = ends[group] - used_frames

    cut = jnp.where(band == 0, used_rows - halo, 0)
    edge = lax.ppermute(
        lax.dynamic_slice_in_dim(latent, cut, halo, 1), "rows", [(0, 1), (1, 0)]
    )
    row_live = (jnp.arange(slots, dtype=jnp.int32) < used_rows)[None, :, None]
    tall = jnp.pad(
        jnp.where(row_live, latent, jnp.zeros_like(latent)), ((0, 0), (halo, halo), (0, 0))
    )
    tall = lax.dynamic_update_slice_in_dim(
        tall, edge, jnp.where(band == 0, used_rows + halo, 0), 1
    )
    right = [(i, i + 1) for i in range(n_cols - 1)]
    left = [(i + 1, i) for i in range(n_cols - 1)]
    low = lax.ppermute(tall[:, :, packed - halo * inner :], "cols", right)
    high = lax.ppermute(tall[:, :, : halo * inner], "cols", left)
    wide = jnp.concatenate([low, tall, high], 2)
    before = [shifted(wide, s) for s in (1, 2, 3)]
    starts = ends - frame_counts
    ids = jnp.arange(n_groups, dtype=jnp.int32)
    third = jnp.maximum(ids - 3, 0)
    short = jnp.any(jnp.logical_and(ids > 3, starts - starts[third] < 6))

    def place(frame):
        owner = jnp.sum((ends <= frame).astype(jnp.int32))
        return (owner - group + 3) * depth + frame - starts[jnp.minimum(owner, n_groups - 1)]

    near = jnp.concatenate(before[::-1] + [wide], 0)

    def further(near):
        frames = [ends[group] - 3 + i for i in range(3)]
        last = jnp.concatenate(
            [
                lax.dynamic_slice_in_dim(near, jnp.clip(place(f), 0, 4 * depth - 1), 1, 0)
                for f in frames
            ],
            0,
        )
        return shifted(last, 4)

    far = lax.cond(short, further, lambda near: jnp.zeros_like(near[:3]), near)
    pool = jnp.concatenate([far, near], 0)
    far_end = starts[jnp.maximum(group - 3, 0)]
    frames = []
    for w in range(6 + depth):
        frame = start - 6 + w
        index = jnp.where(frame < far_end, 3 + frame - far_end, 3 + place(frame))
        if w >= 6:
            index = jnp.int32(3 + 3 * depth + w - 6)
        taken = lax.dynamic_slice_in_dim(pool, jnp.clip(index, 0, 3 + 4 * depth - 1), 1, 0)
        frames.append(jnp.where(frame >= 0, taken, jnp.zeros_like(taken)))
    window = jnp.concatenate(frames, 0)
    tall_slots = slots + 2 * halo
    cells = window.reshape(6 + depth, tall_slots, span + 2 * halo, inner)
    inner_span = span + 4
    trio = jnp.concatenate([cells[:, :, d : d + inner_span] for d in range(3)], -1)
    trio = jnp.pad(trio, ((0, 0), (0, 1), (0, COLS - inner_span), (0, 64 - 3 * inner)))
    x6 = jnp.concatenate([trio[:, :-1], trio[:, 1:]], -1)
    w_in_cat = jnp.pad(
        w_in.reshape(3, 3, 3 * inner, 384), ((0, 0), (0, 1), (0, 64 - 3 * inner), (0, 0))
    ).reshape(768, 384)
    vec = jnp.stack([b_in, 0.5 * gain_one, b_one, 0.5 * gain_two, b_two] + [b_in] * 3)
    info = jnp.stack([used_rows, band, column, start, used_frames]).astype(jnp.int32)
    vmem = pl.BlockSpec(memory_space=pltpu.VMEM)
    return pl.pallas_call(
        functools.partial(kernel, width=span * n_cols, span=span),
        out_shape=jax.ShapeDtypeStruct((depth, slots, span, 384), BF16),
        in_specs=[
            pl.BlockSpec(memory_space=pltpu.SMEM),
            vmem,
            vmem,
            vmem,
            pl.BlockSpec(memory_space=pl.ANY),
            pl.BlockSpec(memory_space=pl.ANY),
        ],
        out_specs=vmem,
        scratch_shapes=[
            pltpu.VMEM((4, 1152, 1152), BF16),
            pltpu.VMEM((4, 1152, 1152), BF16),
            pltpu.VMEM((4, 11, 3, COLS, 384), BF16),
            pltpu.VMEM((4, 10, 2, COLS, 384), BF16),
            pltpu.VMEM((2, 10, 2, COLS, 384), BF16),
            pltpu.SemaphoreType.DMA((2, 27)),
        ],
        compiler_params=pltpu.CompilerParams(vmem_limit_bytes=60 * 2**20),
    )(info, x6, w_in_cat, vec, w_one, w_two)


def solution(mesh):
    placed = (P("stretch", "rows", "cols"), P(), P(), P(), P(), P(), P(), P(), P(), P(), P())
    return jax.shard_map(
        on_device,
        mesh=mesh,
        in_specs=placed,
        out_specs=P("stretch", "rows", "cols", None),
        check_vma=False,
    )
```

```python
import functools

import jax
import jax.numpy as jnp
from jax import lax
from jax.experimental import pallas as pl
from jax.experimental.pallas import tpu as pltpu
from jax.sharding import PartitionSpec as P

F32 = jnp.float32
BF16 = jnp.bfloat16
COLS = 32
SLOT = (0, 1, 3)


def rms_silu(values, half_gain):
    inverse = lax.rsqrt(jnp.mean(values * values, axis=-1, keepdims=True) + 1e-06)
    half = values * inverse * half_gain
    return half + half * jnp.tanh(half)


def weight_copies(source, target, sems):
    copies = []
    for dt in range(3):
        for dh in range(3):
            for dw in range(3):
                copies.append(
                    pltpu.make_async_copy(
                        source.at[dt, dh, dw],
                        target.at[SLOT[dt], pl.ds(dh * 384, 384), pl.ds(dw * 384, 384)],
                        sems.at[dt * 9 + dh * 3 + dw],
                    )
                )
    return copies


def transform_weight(weight):
    step = 64

    def one(i, _):
        rows = pl.ds(pl.multiple_of(i * step, step), step)
        ends = weight[0, rows].astype(F32) + weight[3, rows].astype(F32)
        middle = weight[1, rows].astype(F32)
        weight[1, rows] = (ends + middle).astype(BF16)
        weight[2, rows] = (ends - middle).astype(BF16)
        return 0

    lax.fori_loop(0, weight.shape[1] // step, one, 0)


def store_transformed(target, rows, even, odd, pairs):
    here, after = (slice(0, pairs), slice(1, pairs + 1))
    target[0, rows] = (even[:, here] - even[:, after]).astype(BF16)
    target[1, rows] = (0.5 * (odd[:, here] + even[:, after])).astype(BF16)
    target[2, rows] = (0.5 * (even[:, after] - odd[:, here])).astype(BF16)
    target[3, rows] = (odd[:, here] - odd[:, after]).astype(BF16)


def time_conv(field, weight, start, rows):
    pairs = field.shape[2]
    size = rows * pairs * COLS

    def part(q):
        taps = [
            field[q, pl.ds(start + d, rows)].reshape(size, 384) for d in range(3)
        ]
        return jnp.dot(
            jnp.concatenate(taps, -1), weight[q], preferred_element_type=F32
        )

    def joined(wide):
        return (
            wide[:, :384]
            + pltpu.roll(wide[:, 384:768], size - 1, 0)
            + pltpu.roll(wide[:, 768:], size - 2, 0)
        )

    one, two = part(1), part(2)
    even = joined(part(0) + (one + two))
    odd = joined((one - two) - part(3))
    shape = (rows, pairs, COLS, 384)
    return even.reshape(shape), odd.reshape(shape)


def position(frame_counts):
    group = lax.axis_index("stretch")
    last = frame_counts.shape[0] - 1

    def add(k, total):
        return total + jnp.where(k < group, frame_counts[k], 0)

    start = lax.fori_loop(0, last + 1, add, jnp.int32(0))
    before = []
    for s in (1, 2, 3):
        count = frame_counts[jnp.maximum(group - s, 0)]
        before.append(jnp.where(group >= s, count, 0))
    return frame_counts[group], start, before


def pick(frame, start, before, sources, put):
    end = start
    bounds = [(start, jnp.int32(1 << 20))]
    for count in before:
        bounds.append((end - count, end))
        end = end - count
    bounds.append((end - 3, end))
    for source, (low, high) in zip(sources, bounds):

        @pl.when(jnp.logical_and(jnp.logical_and(frame >= low, frame < high), frame >= 0))
        def _(source=source, low=low):
            put(source[pl.ds(frame - low, 1)])


def tall_kernel(row_counts, frame_counts, own, other, tall, low, high, short):
    band = lax.axis_index("rows")
    used = row_counts[band]
    shape = (own.shape[0], 16, own.shape[2])
    row = lax.broadcasted_iota(jnp.int32, shape, 1)

    def rows16(ref):
        value = ref[...].astype(F32)
        return jnp.concatenate([value, jnp.zeros_like(value)], 1)

    mine = pltpu.roll(rows16(own), 3, 1)
    shift = jnp.where(band == 0, 3 + used, 19 - row_counts[0])
    theirs = pltpu.roll(rows16(other), lax.rem(shift, 16), 1)
    first = jnp.where(band == 0, 3 + used, 0)
    is_mine = jnp.logical_and(row >= 3, row < 3 + used)
    is_theirs = jnp.logical_and(row >= first, row < first + 3)
    value = jnp.where(is_mine, mine, jnp.where(is_theirs, theirs, 0.0)).astype(BF16)
    tall[...] = value
    high[...] = value[:, :, :128]
    low[...] = value[:, :, value.shape[2] - 128 :]

    def lacks(k, found):
        held = frame_counts[k - 1] + frame_counts[k - 2] + frame_counts[k - 3]
        return jnp.where(held < 6, 1, found)

    short[0] = lax.fori_loop(4, frame_counts.shape[0], lacks, jnp.int32(0))


def last_kernel(frame_counts, own, one, two, three, last):
    used, start, before = position(frame_counts)
    for i in range(3):

        def put(slab, i=i):
            last[pl.ds(i, 1)] = slab

        last[pl.ds(i, 1)] = jnp.zeros_like(last[pl.ds(i, 1)])
        pick(start + used - 3 + i, start, before, (own, one, two, three), put)


def kernel(
    row_counts,
    frame_counts,
    own,
    one,
    two,
    three,
    further,
    w_in_ref,
    b_in,
    gain_one,
    b_one,
    gain_two,
    b_two,
    w1_hbm,
    w2_hbm,
    out,
    w1,
    w2,
    v1,
    v2,
    first_s,
    window,
    spread,
    x6,
    w_in,
    sems,
    *,
    width,
    span,
):
    copies1 = weight_copies(w1_hbm, w1, sems.at[0])
    copies2 = weight_copies(w2_hbm, w2, sems.at[1])
    for copy in copies1 + copies2:
        copy.start()
    band = lax.axis_index("rows")
    column = lax.axis_index("cols")
    used_rows = row_counts[band]
    used_frames, start, before = position(frame_counts)

    w_in[...] = jnp.zeros_like(w_in)
    for dt in range(3):
        for dh in range(3):
            w_in[pl.ds(dt * 256 + dh * 64, 48)] = w_in_ref[dt, dh].reshape(48, 384)

    n_frames = window.shape[0]
    window[...] = jnp.zeros_like(window)
    for w in range(n_frames):

        def put(slab, w=w):
            window[pl.ds(w, 1)] = slab.astype(F32)

        if w >= 6:
            put(own[pl.ds(w - 6, 1)])
        else:
            pick(start - 6 + w, start, before, (own, one, two, three, further), put)

    lines = n_frames * 16
    flat = window[...].reshape(lines, window.shape[2])
    spread[...] = jnp.zeros_like(spread)
    for y in range(span + 4):
        piece = flat[:, (y + 5) * 16 : (y + 8) * 16]
        piece = jnp.concatenate([piece, jnp.zeros((lines, 80), F32)], 1)
        spread[pl.ds(y, lines, stride=COLS)] = piece

    def pair_rows(f, _):
        here = spread[pl.ds(pl.multiple_of(f * 16 * COLS, 16 * COLS), 16 * COLS)]
        after = pltpu.roll(here, 15 * COLS, 0)
        both = here + pltpu.roll(after, 64, 1)
        x6[pl.ds(f, 1)] = both.astype(BF16).reshape(1, 16, COLS, 128)
        return 0

    lax.fori_loop(0, n_frames, pair_rows, 0)

    b_in, b_one, b_two = (ref[...].reshape(1, 384) for ref in (b_in, b_one, b_two))
    half_one, half_two = (0.5 * ref[...].reshape(1, 384) for ref in (gain_one, gain_two))
    base_col = column * span

    def inside(shape, axis, shift):
        spot = lax.broadcasted_iota(jnp.int32, shape, axis) + base_col - shift
        return jnp.logical_and(spot >= 0, spot < width)

    zero_row1 = jnp.where(band == 0, 0, used_rows + 2)
    zero_row2 = jnp.where(band == 0, 0, used_rows + 1)
    v1[:, pl.ds(zero_row1, 1)] = jnp.zeros((4, 1, 3, COLS, 384), BF16)

    def in_row(j, _):
        b = j + 2 - 2 * band
        parts = []
        for dt in range(3):
            for dh in (0, 2):
                parts.append(x6[dt : dt + 8, b + dh].reshape(8 * COLS, 128))
        first = jnp.dot(jnp.concatenate(parts, -1), w_in[...], preferred_element_type=F32)
        first = (first + b_in).astype(BF16)
        split = first.reshape(4, 2, COLS, 384)
        for e in range(2):
            first_s[e, j] = split[2:, e]
        act = rms_silu(first.astype(F32), half_one).reshape(8, COLS, 384)
        frame = lax.broadcasted_iota(jnp.int32, (8, COLS, 1), 0) + start - 4
        live = jnp.logical_and(inside((8, COLS, 1), 1, 2), frame >= 0)
        act = jnp.where(live, act, 0.0).reshape(1, 4, 2, COLS, 384)
        store_transformed(v1, pl.ds(j + 1 - band, 1), act[:, :, 0], act[:, :, 1], 3)
        return 0

    lax.fori_loop(0, used_rows + 2, in_row, 0)

    for copy in copies1:
        copy.wait()
    transform_weight(w1)

    def mid_rows(g, _):
        i = g * 3
        even, odd = time_conv(v1, w1, i, 3)
        shape = (3, 3, COLS, 1)
        row = lax.broadcasted_iota(jnp.int32, shape, 0) + i
        frame = 2 * lax.broadcasted_iota(jnp.int32, shape, 1) + start - 2
        live = jnp.logical_and(inside(shape, 2, 1), row <= used_rows)
        acts = []
        for e, y in enumerate((even, odd)):
            act = rms_silu(y + b_one, half_two)
            acts.append(jnp.where(jnp.logical_and(live, frame + e >= 0), act, 0.0))
        store_transformed(v2, pl.ds(i + 1 - band, 3), acts[0], acts[1], 2)
        return 0

    lax.fori_loop(0, (used_rows + 3) // 3, mid_rows, 0)
    v2[:, pl.ds(zero_row2, 1)] = jnp.zeros((4, 1, 2, COLS, 384), BF16)

    for copy in copies2:
        copy.wait()
    transform_weight(w2)

    def out_rows(g, _):
        o = g * 4

        @pl.when(o < used_rows)
        def _():
            parts = time_conv(v2, w2, o, 4)
            row = lax.broadcasted_iota(jnp.int32, (4, COLS, 1), 0) + o
            for e in range(2):
                first = first_s[e, pl.ds(o + 2 * band, 4)].astype(F32)
                first = pltpu.roll(first.reshape(8 * COLS, 384), 8 * COLS - 2, 0)
                total = parts[e] + b_two + first.reshape(4, 2, COLS, 384)
                for p in range(2):
                    live = jnp.logical_and(row < used_rows, 2 * p + e < used_frames)
                    value = jnp.where(live, total[:, p], 0.0).astype(BF16)
                    out[2 * p + e, pl.ds(o, 4)] = value[:, :span]

        @pl.when(o >= used_rows)
        def _():
            out[:, pl.ds(o, 4)] = jnp.zeros((4, 4, span, 384), BF16)

        return 0

    lax.fori_loop(0, 2, out_rows, 0)


def shifted(value, steps):
    count = lax.axis_size("stretch")
    return lax.ppermute(value, "stretch", [(i, i + steps) for i in range(count - steps)])


def on_device(
    latent, frame_counts, row_counts, w_in, b_in, gain_one, w_one, b_one, gain_two, w_two, b_two
):
    depth, slots, packed = latent.shape
    span = packed // w_in.shape[3]
    n_cols = lax.axis_size("cols")
    smem = pl.BlockSpec(memory_space=pltpu.SMEM)
    vmem = pl.BlockSpec(memory_space=pltpu.VMEM)
    anywhere = pl.BlockSpec(memory_space=pl.ANY)

    other = lax.ppermute(latent, "rows", [(0, 1), (1, 0)])
    tall, low, high, short = pl.pallas_call(
        tall_kernel,
        out_shape=[
            jax.ShapeDtypeStruct((depth, 16, packed), BF16),
            jax.ShapeDtypeStruct((depth, 16, 128), BF16),
            jax.ShapeDtypeStruct((depth, 16, 128), BF16),
            jax.ShapeDtypeStruct((1,), jnp.int32),
        ],
        in_specs=[smem, smem, vmem, vmem],
        out_specs=[vmem, vmem, vmem, smem],
        name="tall",
    )(row_counts, frame_counts, latent, other)
    right = [(i, i + 1) for i in range(n_cols - 1)]
    left = [(i + 1, i) for i in range(n_cols - 1)]
    wide = jnp.concatenate(
        [lax.ppermute(low, "cols", right), tall, lax.ppermute(high, "cols", left)], 2
    )
    near = [wide] + [shifted(wide, s) for s in (1, 2, 3)]

    def further_back(near):
        last = pl.pallas_call(
            last_kernel,
            out_shape=jax.ShapeDtypeStruct((3,) + wide.shape[1:], BF16),
            in_specs=[smem] + [vmem] * 4,
            out_specs=vmem,
            name="last",
        )(frame_counts, *near)
        return shifted(last, 4)

    further = lax.cond(
        short[0] > 0, further_back, lambda near: jnp.zeros((3,) + wide.shape[1:], BF16), near
    )
    return pl.pallas_call(
        functools.partial(kernel, width=span * n_cols, span=span),
        out_shape=jax.ShapeDtypeStruct((depth, slots, span, 384), BF16),
        in_specs=[smem, smem] + [vmem] * 11 + [anywhere] * 2,
        out_specs=vmem,
        scratch_shapes=[
            pltpu.VMEM((4, 1152, 1152), BF16),
            pltpu.VMEM((4, 1152, 1152), BF16),
            pltpu.VMEM((4, 11, 3, COLS, 384), BF16),
            pltpu.VMEM((4, 10, 2, COLS, 384), BF16),
            pltpu.VMEM((2, 10, 2, COLS, 384), BF16),
            pltpu.VMEM((6 + depth, 16, wide.shape[2]), F32),
            pltpu.VMEM(((6 + depth) * 16 * COLS, 128), F32),
            pltpu.VMEM((6 + depth, 16, COLS, 128), BF16),
            pltpu.VMEM((768, 384), BF16),
            pltpu.SemaphoreType.DMA((2, 27)),
        ],
        compiler_params=pltpu.CompilerParams(vmem_limit_bytes=60 * 2**20),
        name="block",
    )(row_counts, frame_counts, *near, further, w_in, b_in, gain_one, b_one, gain_two, b_two, w_one, w_two)


def solution(mesh):
    placed = (P("stretch", "rows", "cols"), P(), P(), P(), P(), P(), P(), P(), P(), P(), P())
    return jax.shard_map(
        on_device,
        mesh=mesh,
        in_specs=placed,
        out_specs=P("stretch", "rows", "cols", None),
        check_vma=False,
    )
```

```python
import functools

import jax
import jax.numpy as jnp
from jax import lax
from jax.experimental import pallas as pl
from jax.experimental.pallas import tpu as pltpu
from jax.sharding import PartitionSpec as P

F32 = jnp.float32
BF16 = jnp.bfloat16
COLS = 32
SLOT = (0, 1, 3)


def rms_silu(values, half_gain):
    inverse = lax.rsqrt(jnp.mean(values * values, axis=-1, keepdims=True) + 1e-06)
    half = values * inverse * half_gain
    return half + half * jnp.tanh(half)


def weight_copies(source, target, sems):
    copies = []
    for dt in range(3):
        for dh in range(3):
            for dw in range(3):
                copies.append(
                    pltpu.make_async_copy(
                        source.at[dt, dh, dw],
                        target.at[SLOT[dt], pl.ds(dh * 384, 384), pl.ds(dw * 384, 384)],
                        sems.at[dt * 9 + dh * 3 + dw],
                    )
                )
    return copies


def transform_rows(weight, first, count):
    rows = pl.ds(first, count)
    ends = weight[0, rows] + weight[3, rows]
    middle = weight[1, rows]
    weight[1, rows] = ends + middle
    weight[2, rows] = ends - middle


def transform_weight(weight, start, step):
    def one(i, _):
        transform_rows(weight, pl.multiple_of(i * step, step), step)
        return 0

    lax.fori_loop(start, weight.shape[1] // step, one, 0)


def store_transformed(target, rows, even, odd, pairs):
    here, after = (slice(0, pairs), slice(1, pairs + 1))
    half = jnp.asarray(0.5, BF16)
    target[0, rows] = even[:, here] - even[:, after]
    target[1, rows] = (odd[:, here] + even[:, after]) * half
    target[2, rows] = (even[:, after] - odd[:, here]) * half
    target[3, rows] = odd[:, here] - odd[:, after]


def time_conv(field, weight, start, rows):
    pairs = field.shape[2]
    size = rows * pairs * COLS

    def part(q):
        taps = [
            field[q, pl.ds(start + d, rows)].reshape(size, 384) for d in range(3)
        ]
        return jnp.dot(
            jnp.concatenate(taps, -1), weight[q], preferred_element_type=F32
        )

    def joined(wide):
        return (
            wide[:, :384]
            + pltpu.roll(wide[:, 384:768], size - 1, 0)
            + pltpu.roll(wide[:, 768:], size - 2, 0)
        )

    one, two = part(1), part(2)
    even = joined(part(0) + (one + two))
    odd = joined((one - two) - part(3))
    shape = (rows, pairs, COLS, 384)
    return even.reshape(shape), odd.reshape(shape)


def position(frame_counts):
    group = lax.axis_index("stretch")
    last = frame_counts.shape[0] - 1

    def add(k, total):
        return total + jnp.where(k < group, frame_counts[k], 0)

    start = lax.fori_loop(0, last + 1, add, jnp.int32(0))
    before = []
    for s in (1, 2, 3):
        count = frame_counts[jnp.maximum(group - s, 0)]
        before.append(jnp.where(group >= s, count, 0))
    return frame_counts[group], start, before


def pick(frame, start, before, sources, put):
    end = start
    bounds = [(start, jnp.int32(1 << 20))]
    for count in before:
        bounds.append((end - count, end))
        end = end - count
    bounds.append((end - 3, end))
    for source, (low, high) in zip(sources, bounds):

        @pl.when(jnp.logical_and(jnp.logical_and(frame >= low, frame < high), frame >= 0))
        def _(source=source, low=low):
            put(source[pl.ds(frame - low, 1)])


def last_kernel(frame_counts, own, one, two, three, last):
    used, start, before = position(frame_counts)
    for i in range(3):

        def put(slab, i=i):
            last[pl.ds(i, 1)] = slab

        last[pl.ds(i, 1)] = jnp.zeros_like(last[pl.ds(i, 1)])
        pick(start + used - 3 + i, start, before, (own, one, two, three), put)


def window_kernel(row_counts, frame_counts, own, one, two, three, further, window):
    _, start, before = position(frame_counts)
    live = 16 * row_counts[lax.axis_index("rows")]
    shape = (1,) + window.shape[1:]
    in_use = lax.broadcasted_iota(jnp.int32, shape, 2) < live
    for w in range(window.shape[0]):

        def put(slab, w=w):
            window[pl.ds(w, 1)] = jnp.where(in_use, slab.astype(F32), 0.0).astype(BF16)

        if w >= 6:
            put(own[pl.ds(w - 6, 1)])
        else:
            window[pl.ds(w, 1)] = jnp.zeros(shape, BF16)
            pick(start - 6 + w, start, before, (own, one, two, three, further), put)


def kernel(
    row_counts,
    frame_counts,
    own,
    other,
    low,
    high,
    w_in_ref,
    b_in,
    gain_one,
    b_one,
    gain_two,
    b_two,
    w1_hbm,
    w2_hbm,
    out,
    w1,
    w2,
    v1,
    v2,
    first_s,
    cells,
    patches,
    w_in,
    sems,
    *,
    width,
    span,
):
    copies1 = weight_copies(w1_hbm, w1, sems.at[0])
    copies2 = weight_copies(w2_hbm, w2, sems.at[1])
    for copy in copies1 + copies2:
        copy.start()
    band = lax.axis_index("rows")
    column = lax.axis_index("cols")
    used_rows = row_counts[band]
    used_frames, start, _ = position(frame_counts)

    w_in[...] = jnp.zeros_like(w_in)
    for dt in range(3):
        for dh in range(3):
            for dw in range(3):
                w_in[pl.ds(dt * 256 + dw * 64 + dh * 16, 16)] = w_in_ref[dt, dh, dw]

    shift_own = jnp.where(band == 0, 16, 48)
    shift_other = jnp.where(band == 0, 16 * (used_rows + 1), 256 - 16 * (row_counts[0] - 3))
    lane = lax.broadcasted_iota(jnp.int32, (COLS, 128), 1)

    def frame_patches(f, _):
        def line(ref, side):
            parts = (
                low[pl.ds(f, 1), :, pl.ds(side * 128, 128)],
                ref[pl.ds(f, 1)],
                high[pl.ds(f, 1), :, pl.ds(side * 128, 128)],
            )
            parts = [part.astype(F32).reshape(part.shape[1:]) for part in parts]
            value = jnp.concatenate(parts, 0)
            return jnp.concatenate([value, jnp.zeros_like(value)], 1)

        cells[...] = pltpu.roll(line(own, 0), shift_own, 1) + pltpu.roll(
            line(other, 1), shift_other, 1
        )
        taps = [cells[pl.ds(5 + d, COLS)] for d in range(3)]
        for j in range(patches.shape[1]):
            here = pltpu.roll(taps[0], (256 - 16 * j) % 256, 1)[:, :128]
            beside = pltpu.roll(taps[1], (256 + 64 - 16 * j) % 256, 1)[:, :128]
            far = pltpu.roll(taps[2], (256 - 16 * j) % 256, 1)[:, :128]
            patches[f, j, :, pl.ds(0, 128)] = jnp.where(lane < 64, here, beside).astype(BF16)
            patches[f, j, :, pl.ds(128, 128)] = far.astype(BF16)
        return 0

    lax.fori_loop(0, own.shape[0], frame_patches, 0)

    b_in, b_one, b_two = (ref[...].reshape(1, 384) for ref in (b_in, b_one, b_two))
    half_one, half_two = (0.5 * ref[...].reshape(1, 384) for ref in (gain_one, gain_two))
    base_col = column * span

    def inside(shape, axis, shift):
        spot = lax.broadcasted_iota(jnp.int32, shape, axis) + base_col - shift
        return jnp.logical_and(spot >= 0, spot < width)

    zero_row1 = jnp.where(band == 0, 0, used_rows + 2)
    zero_row2 = jnp.where(band == 0, 0, used_rows + 1)

    def in_row(j):
        parts = [patches[pl.ds(dt, 8), j].reshape(8 * COLS, 256) for dt in range(3)]
        first = jnp.dot(jnp.concatenate(parts, -1), w_in[...], preferred_element_type=F32)
        first = first + b_in
        split = first.reshape(4, 2, COLS, 384)
        for e in range(2):
            first_s[e, j] = split[2:, e].astype(BF16)
        act = rms_silu(first, half_one).reshape(8, COLS, 384)
        frame = lax.broadcasted_iota(jnp.int32, (8, COLS, 1), 0) + start - 4
        live = jnp.logical_and(inside((8, COLS, 1), 1, 2), frame >= 0)
        act = jnp.where(live, act, 0.0).astype(BF16).reshape(1, 4, 2, COLS, 384)
        store_transformed(v1, pl.ds(j + 1 - band, 1), act[:, :, 0], act[:, :, 1], 3)

    def in_rows(i, _):
        for r in range(2):
            in_row(2 * i + r)
        return 0

    lax.fori_loop(0, (used_rows + 3) // 2, in_rows, 0)
    v1[:, pl.ds(zero_row1, 1)] = jnp.zeros((4, 1, 3, COLS, 384), BF16)

    for copy in copies1:
        copy.wait()
    transform_weight(w1, 0, 128)
    for copy in copies2:
        copy.wait()

    def mid_rows(g, _):
        i = g * 3
        even, odd = time_conv(v1, w1, i, 3)
        shape = (3, 3, COLS, 1)
        row = lax.broadcasted_iota(jnp.int32, shape, 0) + i
        frame = 2 * lax.broadcasted_iota(jnp.int32, shape, 1) + start - 2
        live = jnp.logical_and(inside(shape, 2, 1), row <= used_rows)
        acts = []
        for e, y in enumerate((even, odd)):
            act = rms_silu(y + b_one, half_two)
            act = jnp.where(jnp.logical_and(live, frame + e >= 0), act, 0.0)
            acts.append(act.astype(BF16))
        store_transformed(v2, pl.ds(i + 1 - band, 3), acts[0], acts[1], 2)
        transform_rows(w2, pl.multiple_of(g * 384, 384), 384)
        return 0

    groups = (used_rows + 3) // 3
    lax.fori_loop(0, groups, mid_rows, 0)
    transform_weight(w2, groups, 384)
    v2[:, pl.ds(zero_row2, 1)] = jnp.zeros((4, 1, 2, COLS, 384), BF16)

    def out_rows(g, _):
        o = g * 4

        @pl.when(o < used_rows)
        def _():
            parts = time_conv(v2, w2, o, 4)
            row = lax.broadcasted_iota(jnp.int32, (4, COLS, 1), 0) + o
            for e in range(2):
                first = first_s[e, pl.ds(o + 2 * band, 4)].astype(F32)
                first = pltpu.roll(first.reshape(8 * COLS, 384), 8 * COLS - 2, 0)
                total = parts[e] + b_two + first.reshape(4, 2, COLS, 384)
                for p in range(2):
                    live = jnp.logical_and(row < used_rows, 2 * p + e < used_frames)
                    value = jnp.where(live, total[:, p], 0.0).astype(BF16)
                    out[2 * p + e, pl.ds(o, 4)] = value[:, :span]

        @pl.when(o >= used_rows)
        def _():
            out[:, pl.ds(o, 4)] = jnp.zeros((4, 4, span, 384), BF16)

        return 0

    lax.fori_loop(0, 2, out_rows, 0)


def shifted(value, steps):
    count = lax.axis_size("stretch")
    return lax.ppermute(value, "stretch", [(i, i + steps) for i in range(count - steps)])


def on_device(
    latent, frame_counts, row_counts, w_in, b_in, gain_one, w_one, b_one, gain_two, w_two, b_two
):
    depth, slots, packed = latent.shape
    span = packed // w_in.shape[3]
    n_cols = lax.axis_size("cols")
    smem = pl.BlockSpec(memory_space=pltpu.SMEM)
    vmem = pl.BlockSpec(memory_space=pltpu.VMEM)
    anywhere = pl.BlockSpec(memory_space=pl.ANY)
    n_window = 6 + depth

    cells = latent.reshape(depth, slots, span, packed // span)
    cells = cells.transpose(0, 2, 1, 3).reshape(depth, span, slots * packed // span)
    near = [cells] + [shifted(cells, s) for s in (1, 2, 3)]
    held = frame_counts[1:-3] + frame_counts[2:-2] + frame_counts[3:-1]

    def further_back(near):
        last = pl.pallas_call(
            last_kernel,
            out_shape=jax.ShapeDtypeStruct((3,) + cells.shape[1:], BF16),
            in_specs=[smem] + [vmem] * 4,
            out_specs=vmem,
            name="last",
        )(frame_counts, *near)
        return shifted(last, 4)

    further = lax.cond(
        jnp.any(held < 6),
        further_back,
        lambda near: jnp.zeros((3,) + cells.shape[1:], BF16),
        near,
    )
    own = pl.pallas_call(
        window_kernel,
        out_shape=jax.ShapeDtypeStruct((n_window,) + cells.shape[1:], BF16),
        in_specs=[smem, smem] + [vmem] * 5,
        out_specs=vmem,
        name="window",
    )(row_counts, frame_counts, *near, further)
    other = lax.ppermute(own, "rows", [(0, 1), (1, 0)])
    right = [(i, i + 1) for i in range(n_cols - 1)]
    left = [(i + 1, i) for i in range(n_cols - 1)]
    last = jnp.concatenate([own[:, span - 8 :], other[:, span - 8 :]], 2)
    first = jnp.concatenate([own[:, :8], other[:, :8]], 2)
    low = lax.ppermute(last, "cols", right)
    high = lax.ppermute(first, "cols", left)
    return pl.pallas_call(
        functools.partial(kernel, width=span * n_cols, span=span),
        out_shape=jax.ShapeDtypeStruct((depth, slots, span, 384), BF16),
        in_specs=[smem, smem] + [vmem] * 10 + [anywhere] * 2,
        out_specs=vmem,
        scratch_shapes=[
            pltpu.VMEM((4, 1152, 1152), BF16),
            pltpu.VMEM((4, 1152, 1152), BF16),
            pltpu.VMEM((4, 11, 3, COLS, 384), BF16),
            pltpu.VMEM((4, 10, 2, COLS, 384), BF16),
            pltpu.VMEM((2, 10, 2, COLS, 384), BF16),
            pltpu.VMEM((span + 16, 256), F32),
            pltpu.VMEM((n_window, 10, COLS, 256), BF16),
            pltpu.VMEM((768, 384), BF16),
            pltpu.SemaphoreType.DMA((2, 27)),
        ],
        compiler_params=pltpu.CompilerParams(vmem_limit_bytes=60 * 2**20),
        name="block",
    )(
        *(row_counts, frame_counts, own, other, low, high, w_in),
        *(b_in, gain_one, b_one, gain_two, b_two, w_one, w_two),
    )


def solution(mesh):
    placed = (P("stretch", "rows", "cols"), P(), P(), P(), P(), P(), P(), P(), P(), P(), P())
    return jax.shard_map(
        on_device,
        mesh=mesh,
        in_specs=placed,
        out_specs=P("stretch", "rows", "cols", None),
        check_vma=False,
    )
```

```python
import functools

import jax
import jax.numpy as jnp
from jax import lax
from jax.experimental import pallas as pl
from jax.experimental.pallas import tpu as pltpu
from jax.sharding import PartitionSpec as P

F32 = jnp.float32
BF16 = jnp.bfloat16
COLS = 32
SLOT = (0, 1, 3)


def rms_silu(values, half_gain):
    inverse = lax.rsqrt(jnp.mean(values * values, axis=-1, keepdims=True) + 1e-06)
    half = values * inverse * half_gain
    return half + half * jnp.tanh(half)


def weight_copies(source, target, sems):
    copies = []
    for dt in range(3):
        for dh in range(3):
            for dw in range(3):
                copies.append(
                    pltpu.make_async_copy(
                        source.at[dt, dh, dw],
                        target.at[SLOT[dt], pl.ds(dh * 384, 384), pl.ds(dw * 384, 384)],
                        sems.at[dt * 9 + dh * 3 + dw],
                    )
                )
    return copies


def transform_rows(weight, first, count):
    rows = pl.ds(first, count)
    ends = weight[0, rows] + weight[3, rows]
    middle = weight[1, rows]
    weight[1, rows] = ends + middle
    weight[2, rows] = ends - middle


def transform_weight(weight, start, step):
    def one(i, _):
        transform_rows(weight, pl.multiple_of(i * step, step), step)
        return 0

    lax.fori_loop(start, weight.shape[1] // step, one, 0)


def store_transformed(target, rows, even, odd, pairs):
    here, after = (slice(0, pairs), slice(1, pairs + 1))
    half = jnp.asarray(0.5, BF16)
    target[0, rows] = even[:, here] - even[:, after]
    target[1, rows] = (odd[:, here] + even[:, after]) * half
    target[2, rows] = (even[:, after] - odd[:, here]) * half
    target[3, rows] = odd[:, here] - odd[:, after]


def time_conv(field, weight, start, rows):
    pairs = field.shape[2]
    size = rows * pairs * COLS

    def part(q):
        taps = [
            field[q, pl.ds(start + d, rows)].reshape(size, 384) for d in range(3)
        ]
        return jnp.dot(
            jnp.concatenate(taps, -1), weight[q], preferred_element_type=F32
        )

    def joined(wide):
        return (
            wide[:, :384]
            + pltpu.roll(wide[:, 384:768], size - 1, 0)
            + pltpu.roll(wide[:, 768:], size - 2, 0)
        )

    one, two = part(1), part(2)
    even = joined(part(0) + (one + two))
    odd = joined((one - two) - part(3))
    shape = (rows, pairs, COLS, 384)
    return even.reshape(shape), odd.reshape(shape)


def position(frame_counts):
    group = lax.axis_index("stretch")
    last = frame_counts.shape[0] - 1

    def add(k, total):
        return total + jnp.where(k < group, frame_counts[k], 0)

    start = lax.fori_loop(0, last + 1, add, jnp.int32(0))
    before = []
    for s in range(1, 7):
        count = frame_counts[jnp.maximum(group - s, 0)]
        before.append(jnp.where(group >= s, count, 0))
    return frame_counts[group], start, before


def fill_window(window, wide, mine, theirs, start, before, band):
    window[pl.ds(0, 6)] = jnp.zeros((6,) + window.shape[1:], BF16)
    window[pl.ds(6, 4)] = wide[...]

    def halo(w, _):
        frame = start - 6 + w
        end = start
        for d, count in enumerate(before):
            low = end - count
            slot = frame - low if d < 4 else frame - end + 2
            held = jnp.logical_and(jnp.logical_and(frame >= low, frame < end), frame >= 0)
            end = low

            @pl.when(jnp.logical_and(held, band == d % 2))
            def _(slot=slot, source=mine[d // 2]):
                window[pl.ds(w, 1)] = source[pl.ds(slot, 1)]

            @pl.when(jnp.logical_and(held, band != d % 2))
            def _(slot=slot, source=theirs[d // 2]):
                slab = source[pl.ds(slot, 1)]
                window[pl.ds(w, 1)] = jnp.concatenate([slab[:, :, 128:], slab[:, :, :128]], 2)

        return 0

    lax.fori_loop(0, 6, halo, 0)


def kernel(
    row_counts,
    frame_counts,
    wide,
    near,
    far,
    furthest,
    near_other,
    far_other,
    w_in_ref,
    b_in,
    gain_one,
    b_one,
    gain_two,
    b_two,
    w1_hbm,
    w2_hbm,
    out,
    w1,
    w2,
    v1,
    v2,
    first_s,
    window,
    cells,
    patches,
    w_in,
    sems,
    *,
    width,
    span,
):
    copies1 = weight_copies(w1_hbm, w1, sems.at[0])
    copies2 = weight_copies(w2_hbm, w2, sems.at[1])
    for copy in copies1 + copies2:
        copy.start()
    band = lax.axis_index("rows")
    column = lax.axis_index("cols")
    used_rows = row_counts[band]
    used_frames, start, before = position(frame_counts)

    w_in[...] = jnp.zeros_like(w_in)
    for dt in range(3):
        for dh in range(3):
            for dw in range(3):
                w_in[pl.ds(dt * 256 + dw * 64 + dh * 16, 16)] = w_in_ref[dt, dh, dw]

    mine = (near, far, furthest)
    theirs = (near_other, far_other, furthest.at[pl.ds(2, 2)])
    fill_window(window, wide, mine, theirs, start, before, band)

    shift_own = jnp.where(band == 0, 16, 48)
    shift_other = jnp.where(band == 0, 16 * (used_rows + 1), 256 - 16 * (row_counts[0] - 3))
    lane = lax.broadcasted_iota(jnp.int32, (COLS, 128), 1)
    wide_lane = lax.broadcasted_iota(jnp.int32, (wide.shape[1], 128), 1)

    def frame_patches(f, _):
        both = window[f].astype(F32)

        def line(value, rows):
            value = jnp.where(wide_lane < 16 * rows, value, 0.0)
            return jnp.concatenate([value, jnp.zeros_like(value)], 1)

        cells[...] = pltpu.roll(line(both[:, :128], used_rows), shift_own, 1) + pltpu.roll(
            line(both[:, 128:], row_counts[1 - band]), shift_other, 1
        )
        taps = [cells[pl.ds(5 + d, COLS)] for d in range(3)]
        for j in range(patches.shape[1]):
            here = pltpu.roll(taps[0], (256 - 16 * j) % 256, 1)[:, :128]
            beside = pltpu.roll(taps[1], (256 + 64 - 16 * j) % 256, 1)[:, :128]
            far = pltpu.roll(taps[2], (256 - 16 * j) % 256, 1)[:, :128]
            patches[f, j, :, pl.ds(0, 128)] = jnp.where(lane < 64, here, beside).astype(BF16)
            patches[f, j, :, pl.ds(128, 128)] = far.astype(BF16)
        return 0

    lax.fori_loop(0, window.shape[0], frame_patches, 0)

    b_in, b_one, b_two = (ref[...].reshape(1, 384) for ref in (b_in, b_one, b_two))
    half_one, half_two = (0.5 * ref[...].reshape(1, 384) for ref in (gain_one, gain_two))
    base_col = column * span

    def inside(shape, axis, shift):
        spot = lax.broadcasted_iota(jnp.int32, shape, axis) + base_col - shift
        return jnp.logical_and(spot >= 0, spot < width)

    zero_row1 = jnp.where(band == 0, 0, used_rows + 2)
    zero_row2 = jnp.where(band == 0, 0, used_rows + 1)

    def in_row(j):
        parts = [patches[pl.ds(dt, 8), j].reshape(8 * COLS, 256) for dt in range(3)]
        first = jnp.dot(jnp.concatenate(parts, -1), w_in[...], preferred_element_type=F32)
        first = first + b_in
        split = first.reshape(4, 2, COLS, 384)
        for e in range(2):
            first_s[e, j] = split[2:, e].astype(BF16)
        act = rms_silu(first, half_one).reshape(8, COLS, 384)
        frame = lax.broadcasted_iota(jnp.int32, (8, COLS, 1), 0) + start - 4
        live = jnp.logical_and(inside((8, COLS, 1), 1, 2), frame >= 0)
        act = jnp.where(live, act, 0.0).astype(BF16).reshape(1, 4, 2, COLS, 384)
        store_transformed(v1, pl.ds(j + 1 - band, 1), act[:, :, 0], act[:, :, 1], 3)

    def in_rows(i, _):
        for r in range(2):
            in_row(2 * i + r)
        return 0

    lax.fori_loop(0, (used_rows + 3) // 2, in_rows, 0)
    v1[:, pl.ds(zero_row1, 1)] = jnp.zeros((4, 1, 3, COLS, 384), BF16)

    for copy in copies1:
        copy.wait()
    transform_weight(w1, 0, 128)
    for copy in copies2:
        copy.wait()

    def mid_rows(g, _):
        i = g * 3
        even, odd = time_conv(v1, w1, i, 3)
        shape = (3, 3, COLS, 1)
        row = lax.broadcasted_iota(jnp.int32, shape, 0) + i
        frame = 2 * lax.broadcasted_iota(jnp.int32, shape, 1) + start - 2
        live = jnp.logical_and(inside(shape, 2, 1), row <= used_rows)
        acts = []
        for e, y in enumerate((even, odd)):
            act = rms_silu(y + b_one, half_two)
            act = jnp.where(jnp.logical_and(live, frame + e >= 0), act, 0.0)
            acts.append(act.astype(BF16))
        store_transformed(v2, pl.ds(i + 1 - band, 3), acts[0], acts[1], 2)
        transform_rows(w2, pl.multiple_of(g * 384, 384), 384)
        return 0

    groups = (used_rows + 3) // 3
    lax.fori_loop(0, groups, mid_rows, 0)
    transform_weight(w2, groups, 384)
    v2[:, pl.ds(zero_row2, 1)] = jnp.zeros((4, 1, 2, COLS, 384), BF16)

    def out_rows(g, _):
        o = g * 4

        @pl.when(o < used_rows)
        def _():
            parts = time_conv(v2, w2, o, 4)
            row = lax.broadcasted_iota(jnp.int32, (4, COLS, 1), 0) + o
            for e in range(2):
                first = first_s[e, pl.ds(o + 2 * band, 4)].astype(F32)
                first = pltpu.roll(first.reshape(8 * COLS, 384), 8 * COLS - 2, 0)
                total = parts[e] + b_two + first.reshape(4, 2, COLS, 384)
                for p in range(2):
                    live = jnp.logical_and(row < used_rows, 2 * p + e < used_frames)
                    value = jnp.where(live, total[:, p], 0.0).astype(BF16)
                    out[2 * p + e, pl.ds(o, 4)] = value[:, :span]

        @pl.when(o >= used_rows)
        def _():
            out[:, pl.ds(o, 4)] = jnp.zeros((4, 4, span, 384), BF16)

        return 0

    lax.fori_loop(0, 2, out_rows, 0)


def from_before(value, steps):
    count = lax.axis_size("stretch")
    pairs = [
        (k * 2 + j, (k + steps + j) * 2 + j) for j in range(2) for k in range(count - steps - j)
    ]
    return lax.ppermute(value, ("stretch", "rows"), pairs)


def swapped(value):
    return lax.ppermute(value, "rows", [(0, 1), (1, 0)])


def on_device(
    latent, frame_counts, row_counts, w_in, b_in, gain_one, w_one, b_one, gain_two, w_two, b_two
):
    depth, slots, packed = latent.shape
    span = packed // w_in.shape[3]
    n_cols = lax.axis_size("cols")
    smem = pl.BlockSpec(memory_space=pltpu.SMEM)
    vmem = pl.BlockSpec(memory_space=pltpu.VMEM)
    anywhere = pl.BlockSpec(memory_space=pl.ANY)
    n_window = 6 + depth

    cells = latent.reshape(depth, slots, span, packed // span)
    cells = cells.transpose(0, 2, 1, 3).reshape(depth, span, slots * packed // span)
    cells = jnp.concatenate([cells, swapped(cells)], 2)
    right = [(i, i + 1) for i in range(n_cols - 1)]
    left = [(i + 1, i) for i in range(n_cols - 1)]
    low = lax.ppermute(cells[:, span - 8 :], "cols", right)
    high = lax.ppermute(cells[:, :8], "cols", left)
    wide = jnp.concatenate([low, cells, high], 1)
    held = sum(frame_counts[i : i - 5] for i in range(1, 5))
    wide, short = lax.optimization_barrier((wide, jnp.any(held < 6)))
    near, far = from_before(wide, 1), from_before(wide, 3)
    near_other, far_other = swapped(near), swapped(far)

    def further_back(wide):
        used = frame_counts[lax.axis_index("stretch")]
        last = lax.dynamic_slice_in_dim(jnp.pad(wide, ((2, 0), (0, 0), (0, 0))), used, 2, 0)
        found = from_before(last, 5)
        return jnp.concatenate([found, swapped(found)], 0)

    furthest = lax.cond(short, further_back, lambda wide: jnp.zeros_like(wide), wide)
    return pl.pallas_call(
        functools.partial(kernel, width=span * n_cols, span=span),
        out_shape=jax.ShapeDtypeStruct((depth, slots, span, 384), BF16),
        in_specs=[smem, smem] + [vmem] * 12 + [anywhere] * 2,
        out_specs=vmem,
        scratch_shapes=[
            pltpu.VMEM((4, 1152, 1152), BF16),
            pltpu.VMEM((4, 1152, 1152), BF16),
            pltpu.VMEM((4, 11, 3, COLS, 384), BF16),
            pltpu.VMEM((4, 10, 2, COLS, 384), BF16),
            pltpu.VMEM((2, 10, 2, COLS, 384), BF16),
            pltpu.VMEM((n_window, span + 16, 256), BF16),
            pltpu.VMEM((span + 16, 256), F32),
            pltpu.VMEM((n_window, 10, COLS, 256), BF16),
            pltpu.VMEM((768, 384), BF16),
            pltpu.SemaphoreType.DMA((2, 27)),
        ],
        compiler_params=pltpu.CompilerParams(vmem_limit_bytes=57 * 2**20),
        name="block",
    )(
        *(row_counts, frame_counts, wide, near, far, furthest),
        *(near_other, far_other, w_in),
        *(b_in, gain_one, b_one, gain_two, b_two, w_one, w_two),
    )


def solution(mesh):
    placed = (P("stretch", "rows", "cols"), P(), P(), P(), P(), P(), P(), P(), P(), P(), P())
    return jax.shard_map(
        on_device,
        mesh=mesh,
        in_specs=placed,
        out_specs=P("stretch", "rows", "cols", None),
        check_vma=False,
    )
```

```python
import functools

import jax
import jax.numpy as jnp
from jax import lax
from jax.experimental import pallas as pl
from jax.experimental.pallas import tpu as pltpu
from jax.sharding import PartitionSpec as P

F32 = jnp.float32
BF16 = jnp.bfloat16
COLS = 32
SLOT = (0, 1, 3)


def rms_silu(values, half_gain, live):
    inverse = lax.rsqrt(jnp.mean(values * values, axis=-1, keepdims=True) + 1e-06)
    half = values * jnp.where(live, inverse, 0.0) * half_gain
    return half + half * jnp.tanh(half)


def weight_copies(source, target, sems):
    copies = []
    for dt in range(3):
        for dh in range(3):
            for dw in range(3):
                copies.append(
                    pltpu.make_async_copy(
                        source.at[dt, dh, dw],
                        target.at[SLOT[dt], pl.ds(dh * 384, 384), pl.ds(dw * 384, 384)],
                        sems.at[dt * 9 + dh * 3 + dw],
                    )
                )
    return copies


def transform_rows(weight, first, count):
    rows = pl.ds(first, count)
    ends = weight[0, rows] + weight[3, rows]
    middle = weight[1, rows]
    weight[1, rows] = ends + middle
    weight[2, rows] = ends - middle


def transform_weight(weight, start, step):
    def one(i, _):
        transform_rows(weight, pl.multiple_of(i * step, step), step)
        return 0

    lax.fori_loop(start, weight.shape[1] // step, one, 0)


def height_copies(source, target, sems, dh):
    return [
        pltpu.make_async_copy(source.at[dt, dh], target.at[SLOT[dt], dh], sems.at[dt * 3 + dh])
        for dt in range(3)
    ]


def store_transformed(target, rows, even, odd, pairs, lanes=pl.ds(0, 384)):
    here, after = (slice(0, pairs), slice(1, pairs + 1))
    half = jnp.asarray(0.5, BF16)
    target[0, rows, :, :, lanes] = even[:, here] - even[:, after]
    target[1, rows, :, :, lanes] = (odd[:, here] + even[:, after]) * half
    target[2, rows, :, :, lanes] = (even[:, after] - odd[:, here]) * half
    target[3, rows, :, :, lanes] = odd[:, here] - odd[:, after]


def time_conv(field, weight, start, rows):
    pairs = field.shape[2]
    size = rows * pairs * COLS

    def part(q):
        taps = [
            field[q, pl.ds(start + d, rows)].reshape(size, 384) for d in range(3)
        ]
        return jnp.dot(
            jnp.concatenate(taps, -1), weight[q], preferred_element_type=F32
        )

    def joined(wide):
        return (
            wide[:, :384]
            + pltpu.roll(wide[:, 384:768], size - 1, 0)
            + pltpu.roll(wide[:, 768:], size - 2, 0)
        )

    one, two = part(1), part(2)
    even = joined(part(0) + (one + two))
    odd = joined((one - two) - part(3))
    shape = (rows, pairs, COLS, 384)
    return even.reshape(shape), odd.reshape(shape)


def position(frame_counts):
    group = lax.axis_index("stretch")
    last = frame_counts.shape[0] - 1

    def add(k, total):
        return total + jnp.where(k < group, frame_counts[k], 0)

    start = lax.fori_loop(0, last + 1, add, jnp.int32(0))
    before = []
    for s in range(1, 7):
        count = frame_counts[jnp.maximum(group - s, 0)]
        before.append(jnp.where(group >= s, count, 0))
    return frame_counts[group], start, before


def fill_window(window, wide, mine, theirs, start, before, band):
    window[pl.ds(0, 6)] = jnp.zeros((6,) + window.shape[1:], BF16)
    window[pl.ds(6, 4)] = wide[...]

    def halo(w, _):
        frame = start - 6 + w
        end = start
        for d, count in enumerate(before):
            low = end - count
            slot = frame - low if d < 4 else frame - end + 2
            held = jnp.logical_and(jnp.logical_and(frame >= low, frame < end), frame >= 0)
            end = low

            @pl.when(jnp.logical_and(held, band == d % 2))
            def _(slot=slot, source=mine[d // 2]):
                window[pl.ds(w, 1)] = source[pl.ds(slot, 1)]

            @pl.when(jnp.logical_and(held, band != d % 2))
            def _(slot=slot, source=theirs[d // 2]):
                slab = source[pl.ds(slot, 1)]
                window[pl.ds(w, 1)] = jnp.concatenate([slab[:, :, 128:], slab[:, :, :128]], 2)

        return 0

    lax.fori_loop(0, 6, halo, 0)


def kernel(
    row_counts,
    frame_counts,
    wide,
    near,
    far,
    furthest,
    near_other,
    far_other,
    w_in_ref,
    b_in,
    gain_one,
    b_one,
    gain_two,
    b_two,
    w1_hbm,
    w2_hbm,
    out,
    w1,
    w2,
    v1,
    v2,
    first_s,
    window,
    cells,
    w_in,
    sums,
    sems,
    sems2,
    *,
    width,
    span,
):
    copies1 = weight_copies(w1_hbm, w1, sems)
    for copy in copies1:
        copy.start()
    for dh in range(3):
        for copy in height_copies(w2_hbm, w2, sems2, dh):
            copy.start()
    band = lax.axis_index("rows")
    column = lax.axis_index("cols")
    used_rows = row_counts[band]
    used_frames, start, before = position(frame_counts)

    w_in[...] = jnp.zeros_like(w_in)
    for dt in range(3):
        for dh in range(3):
            for dw in range(3):
                w_in[pl.ds(dt * 256 + dw * 64 + dh * 16, 16)] = w_in_ref[dt, dh, dw]

    mine = (near, far, furthest)
    theirs = (near_other, far_other, furthest.at[pl.ds(2, 2)])
    fill_window(window, wide, mine, theirs, start, before, band)

    shift_own = jnp.where(band == 0, 16, 48)
    shift_other = jnp.where(band == 0, 16 * (used_rows + 1), 256 - 16 * (row_counts[0] - 3))
    lane = lax.broadcasted_iota(jnp.int32, (COLS, 128), 1)
    wide_lane = lax.broadcasted_iota(jnp.int32, (wide.shape[1], 128), 1)

    def frame_cells(f, _):
        both = window[f].astype(F32)

        def line(value, rows):
            value = jnp.where(wide_lane < 16 * rows, value, 0.0)
            return jnp.concatenate([value, jnp.zeros_like(value)], 1)

        cells[f] = pltpu.roll(line(both[:, :128], used_rows), shift_own, 1) + pltpu.roll(
            line(both[:, 128:], row_counts[1 - band]), shift_other, 1
        )
        return 0

    lax.fori_loop(0, window.shape[0], frame_cells, 0)

    b_in, b_one, b_two = (ref[...].reshape(1, 384) for ref in (b_in, b_one, b_two))
    half_one, half_two = (0.5 * ref[...].reshape(1, 384) for ref in (gain_one, gain_two))
    base_col = column * span

    def inside(shape, axis, shift):
        spot = lax.broadcasted_iota(jnp.int32, shape, axis) + base_col - shift
        return jnp.logical_and(spot >= 0, spot < width)

    zero_row1 = jnp.where(band == 0, 0, used_rows + 2)
    zero_row2 = jnp.where(band == 0, 0, used_rows + 1)

    def in_row(j):
        shift = lax.rem(256 - 16 * j, 256)
        beside = lax.rem(256 + 64 - 16 * j, 256)
        frames = []
        for f in range(cells.shape[0]):
            taps = [
                pltpu.roll(cells[f, pl.ds(5 + d, COLS)], beside if d == 1 else shift, 1)[:, :128]
                for d in range(3)
            ]
            frames.append(
                jnp.concatenate([jnp.where(lane < 64, taps[0], taps[1]), taps[2]], 1).astype(BF16)
            )
        parts = [jnp.concatenate(frames[dt : dt + 8], 0) for dt in range(3)]
        first = jnp.dot(jnp.concatenate(parts, -1), w_in[...], preferred_element_type=F32)
        first = first + b_in
        split = first.reshape(4, 2, COLS, 384)
        for e in range(2):
            first_s[e, j] = split[2:, e].astype(BF16)
        frame = lax.broadcasted_iota(jnp.int32, (8, COLS, 1), 0) + start - 4
        live = jnp.logical_and(inside((8, COLS, 1), 1, 2), frame >= 0)
        act = rms_silu(first.reshape(8, COLS, 384), half_one, live)
        act = act.astype(BF16).reshape(1, 4, 2, COLS, 384)
        store_transformed(v1, pl.ds(j + 1 - band, 1), act[:, :, 0], act[:, :, 1], 3)

    def in_rows(i, _):
        for r in range(2):
            in_row(2 * i + r)
        return 0

    lax.fori_loop(0, (used_rows + 3) // 2, in_rows, 0)
    v1[:, pl.ds(zero_row1, 1)] = jnp.zeros((4, 1, 3, COLS, 384), BF16)

    for copy in copies1:
        copy.wait()
    transform_weight(w1, 0, 128)

    def next_weight(g):
        for copy in height_copies(w2_hbm, w2, sems2, g):
            copy.wait()

    def mid_rows(i, count):
        size = count * 3 * COLS
        shape = (count, 3, COLS, 1)
        frame = 2 * lax.broadcasted_iota(jnp.int32, shape, 1) + start - 2
        column_live = inside(shape, 2, 1)
        acts = []
        for e, value in enumerate(time_conv(v1, w1, i, count)):
            live = jnp.logical_and(column_live, frame + e >= 0)
            acts.append(rms_silu(value + b_one, half_two, live).reshape(size, 384))
        for d in range(3):
            even, odd = (
                pltpu.roll(act, (size - d) % size, 0)
                .reshape(count, 3, COLS, 384)[:, :, :span]
                .astype(BF16)
                for act in acts
            )
            store_transformed(
                v2, pl.ds(i + 1 - band, count), even, odd, 2, pl.ds(d * 384, 384)
            )

    def fours(g, _):
        next_weight(g)
        mid_rows(4 * g, 4)
        transform_rows(w2, g, 1)
        return 0

    def threes(g, _):
        next_weight(n_fours + g)
        mid_rows(4 * n_fours + 3 * g, 3)
        transform_rows(w2, n_fours + g, 1)
        return 0

    def late_weight(g, _):
        next_weight(g)
        transform_rows(w2, g, 1)
        return 0

    n_fours = jnp.where(used_rows == 6, 1, jnp.where(used_rows == 7, 2, 0))
    n_threes = jnp.where(used_rows == 8, 3, jnp.where(used_rows == 7, 0, jnp.where(used_rows == 6, 1, 2)))
    lax.fori_loop(0, n_fours, fours, 0)
    lax.fori_loop(0, n_threes, threes, 0)
    lax.fori_loop(n_fours + n_threes, 3, late_weight, 0)
    v2[:, pl.ds(zero_row2, 1)] = jnp.zeros((4, 1) + v2.shape[2:], BF16)

    def out_rows(count):
        size = count * 2 * span
        sums[...] = jnp.zeros_like(sums)

        def out_part(q, _):
            taps = [v2[q, pl.ds(d, count)].reshape(size, 1152) for d in range(3)]
            value = jnp.dot(
                jnp.concatenate(taps, -1), w2[q].reshape(3456, 384), preferred_element_type=F32
            )
            used = pl.ds(0, size)
            sums[0, used] += jnp.where(q < 3, 1.0, 0.0) * value
            sums[1, used] += jnp.where(q == 0, 0.0, jnp.where(q == 1, 1.0, -1.0)) * value
            return 0

        lax.fori_loop(0, 4, out_part, 0)

    @pl.when(used_rows > 6)
    def _():
        out_rows(8)

    @pl.when(used_rows <= 6)
    def _():
        out_rows(6)

    row = lax.broadcasted_iota(jnp.int32, (8, span, 1), 0)
    for e in range(2):
        first = first_s[e, pl.ds(2 * band, 8)].astype(F32).reshape(16 * COLS, 384)
        first = pltpu.roll(first, 16 * COLS - 2, 0).reshape(8, 2, COLS, 384)[:, :, :span]
        total = sums[e].reshape(8, 2, span, 384) + b_two + first
        for p in range(2):
            live = jnp.logical_and(row < used_rows, 2 * p + e < used_frames)
            out[2 * p + e] = jnp.where(live, total[:, p], 0.0).astype(BF16)


def from_before(value, steps):
    count = lax.axis_size("stretch")
    pairs = [
        (k * 2 + j, (k + steps + j) * 2 + j) for j in range(2) for k in range(count - steps - j)
    ]
    return lax.ppermute(value, ("stretch", "rows"), pairs)


def swapped(value):
    return lax.ppermute(value, "rows", [(0, 1), (1, 0)])


def on_device(
    latent, frame_counts, row_counts, w_in, b_in, gain_one, w_one, b_one, gain_two, w_two, b_two
):
    depth, slots, packed = latent.shape
    span = packed // w_in.shape[3]
    n_cols = lax.axis_size("cols")
    smem = pl.BlockSpec(memory_space=pltpu.SMEM)
    vmem = pl.BlockSpec(memory_space=pltpu.VMEM)
    anywhere = pl.BlockSpec(memory_space=pl.ANY)
    n_window = 6 + depth

    cells = latent.reshape(depth, slots, span, packed // span)
    cells = cells.transpose(0, 2, 1, 3).reshape(depth, span, slots * packed // span)
    cells = jnp.concatenate([cells, swapped(cells)], 2)
    right = [(i, i + 1) for i in range(n_cols - 1)]
    left = [(i + 1, i) for i in range(n_cols - 1)]
    low = lax.ppermute(cells[:, span - 8 :], "cols", right)
    high = lax.ppermute(cells[:, :8], "cols", left)
    wide = jnp.concatenate([low, cells, high], 1)
    held = sum(frame_counts[i : i - 5] for i in range(1, 5))
    wide, short = lax.optimization_barrier((wide, jnp.any(held < 6)))
    near, far = from_before(wide, 1), from_before(wide, 3)
    near_other, far_other = swapped(near), swapped(far)

    def further_back(wide):
        used = frame_counts[lax.axis_index("stretch")]
        last = lax.dynamic_slice_in_dim(jnp.pad(wide, ((2, 0), (0, 0), (0, 0))), used, 2, 0)
        found = from_before(last, 5)
        return jnp.concatenate([found, swapped(found)], 0)

    furthest = lax.cond(short, further_back, lambda wide: jnp.zeros_like(wide), wide)
    return pl.pallas_call(
        functools.partial(kernel, width=span * n_cols, span=span),
        out_shape=jax.ShapeDtypeStruct((depth, slots, span, 384), BF16),
        in_specs=[smem, smem] + [vmem] * 12 + [anywhere] * 2,
        out_specs=vmem,
        scratch_shapes=[
            pltpu.VMEM((4, 1152, 1152), BF16),
            pltpu.VMEM((4, 3, 3, 384, 384), BF16),
            pltpu.VMEM((4, 11, 3, COLS, 384), BF16),
            pltpu.VMEM((4, 10, 2, span, 1152), BF16),
            pltpu.VMEM((2, 10, 2, COLS, 384), BF16),
            pltpu.VMEM((n_window, span + 16, 256), BF16),
            pltpu.VMEM((n_window, span + 16, 256), F32),
            pltpu.VMEM((768, 384), BF16),
            pltpu.VMEM((2, 16 * span, 384), F32),
            pltpu.SemaphoreType.DMA((27,)),
            pltpu.SemaphoreType.DMA((9,)),
        ],
        compiler_params=pltpu.CompilerParams(vmem_limit_bytes=57 * 2**20),
        name="block",
    )(
        *(row_counts, frame_counts, wide, near, far, furthest),
        *(near_other, far_other, w_in),
        *(b_in, gain_one, b_one, gain_two, b_two, w_one, w_two),
    )


def solution(mesh):
    placed = (P("stretch", "rows", "cols"), P(), P(), P(), P(), P(), P(), P(), P(), P(), P())
    return jax.shard_map(
        on_device,
        mesh=mesh,
        in_specs=placed,
        out_specs=P("stretch", "rows", "cols", None),
        check_vma=False,
    )
```

```python
import functools

import jax
import jax.numpy as jnp
from jax import lax
from jax.experimental import pallas as pl
from jax.experimental.pallas import tpu as pltpu
from jax.sharding import PartitionSpec as P

F32 = jnp.float32
BF16 = jnp.bfloat16
COLS = 32
SLOT = (0, 1, 3)


def rms_silu(values, half_gain, live):
    inverse = lax.rsqrt(jnp.mean(values * values, axis=-1, keepdims=True) + 1e-06)
    half = values * jnp.where(live, inverse, 0.0) * half_gain
    return half + half * jnp.tanh(half)


def weight_copies(source, target, sems):
    copies = []
    for dt in range(3):
        for dh in range(3):
            for dw in range(3):
                copies.append(
                    pltpu.make_async_copy(
                        source.at[dt, dh, dw],
                        target.at[SLOT[dt], pl.ds(dh * 384, 384), pl.ds(dw * 384, 384)],
                        sems.at[dt * 9 + dh * 3 + dw],
                    )
                )
    return copies


def transform_rows(weight, first, count):
    rows = pl.ds(first, count)
    ends = weight[0, rows] + weight[3, rows]
    middle = weight[1, rows]
    weight[1, rows] = ends + middle
    weight[2, rows] = ends - middle


def transform_weight(weight, start, step):
    def one(i, _):
        transform_rows(weight, pl.multiple_of(i * step, step), step)
        return 0

    lax.fori_loop(start, weight.shape[1] // step, one, 0)


def height_copies(source, target, sems, dh):
    return [
        pltpu.make_async_copy(source.at[dt, dh], target.at[SLOT[dt], dh], sems.at[dt * 3 + dh])
        for dt in range(3)
    ]


def store_transformed(target, rows, even, odd, pairs, lanes=pl.ds(0, 384)):
    here, after = (slice(0, pairs), slice(1, pairs + 1))
    half = jnp.asarray(0.5, BF16)
    target[0, rows, :, :, lanes] = even[:, here] - even[:, after]
    target[1, rows, :, :, lanes] = (odd[:, here] + even[:, after]) * half
    target[2, rows, :, :, lanes] = (even[:, after] - odd[:, here]) * half
    target[3, rows, :, :, lanes] = odd[:, here] - odd[:, after]


def time_conv(field, weight, start, rows):
    pairs = field.shape[2]
    size = rows * pairs * COLS

    def part(q):
        taps = [
            field[q, pl.ds(start + d, rows)].reshape(size, 384) for d in range(3)
        ]
        return jnp.dot(
            jnp.concatenate(taps, -1), weight[q], preferred_element_type=F32
        )

    def joined(wide):
        return (
            wide[:, :384]
            + pltpu.roll(wide[:, 384:768], size - 1, 0)
            + pltpu.roll(wide[:, 768:], size - 2, 0)
        )

    one, two = part(1), part(2)
    even = joined(part(0) + (one + two))
    odd = joined((one - two) - part(3))
    shape = (rows, pairs, COLS, 384)
    return even.reshape(shape), odd.reshape(shape)


def position(frame_counts):
    group = lax.axis_index("stretch")
    last = frame_counts.shape[0] - 1

    def add(k, total):
        return total + jnp.where(k < group, frame_counts[k], 0)

    start = lax.fori_loop(0, last + 1, add, jnp.int32(0))
    before = []
    for s in range(1, 7):
        count = frame_counts[jnp.maximum(group - s, 0)]
        before.append(jnp.where(group >= s, count, 0))
    return frame_counts[group], start, before


def fill_window(window, wide, mine, theirs, start, before, band):
    window[pl.ds(0, 6)] = jnp.zeros((6,) + window.shape[1:], BF16)
    window[pl.ds(6, 4)] = wide[...]

    def halo(w, _):
        frame = start - 6 + w
        end = start
        for d, count in enumerate(before):
            low = end - count
            slot = frame - low if d < 4 else frame - end + 2
            held = jnp.logical_and(jnp.logical_and(frame >= low, frame < end), frame >= 0)
            end = low

            @pl.when(jnp.logical_and(held, band == d % 2))
            def _(slot=slot, source=mine[d // 2]):
                window[pl.ds(w, 1)] = source[pl.ds(slot, 1)]

            @pl.when(jnp.logical_and(held, band != d % 2))
            def _(slot=slot, source=theirs[d // 2]):
                slab = source[pl.ds(slot, 1)]
                window[pl.ds(w, 1)] = jnp.concatenate([slab[:, :, 128:], slab[:, :, :128]], 2)

        return 0

    lax.fori_loop(0, 6, halo, 0)


def kernel(
    row_counts,
    frame_counts,
    wide,
    near,
    far,
    furthest,
    near_other,
    far_other,
    w_in_ref,
    b_in,
    gain_one,
    b_one,
    gain_two,
    b_two,
    w1_hbm,
    w2_hbm,
    out,
    w1,
    w2,
    v1,
    v2,
    first_s,
    window,
    cells,
    w_in,
    acts,
    sums,
    sems,
    sems2,
    *,
    width,
    span,
):
    copies1 = weight_copies(w1_hbm, w1, sems)
    for copy in copies1:
        copy.start()
    for dh in range(3):
        for copy in height_copies(w2_hbm, w2, sems2, dh):
            copy.start()
    band = lax.axis_index("rows")
    column = lax.axis_index("cols")
    used_rows = row_counts[band]
    used_frames, start, before = position(frame_counts)

    w_in[...] = jnp.zeros_like(w_in)
    for dt in range(3):
        for dh in range(3):
            for dw in range(3):
                w_in[pl.ds(dt * 256 + dw * 64 + dh * 16, 16)] = w_in_ref[dt, dh, dw]

    mine = (near, far, furthest)
    theirs = (near_other, far_other, furthest.at[pl.ds(2, 2)])
    fill_window(window, wide, mine, theirs, start, before, band)

    shift_own = jnp.where(band == 0, 16, 48)
    shift_other = jnp.where(band == 0, 16 * (used_rows + 1), 256 - 16 * (row_counts[0] - 3))
    lane = lax.broadcasted_iota(jnp.int32, (COLS, 128), 1)
    wide_lane = lax.broadcasted_iota(jnp.int32, (wide.shape[1], 128), 1)

    def frame_cells(f):
        both = window[f].astype(F32)

        def line(value, rows):
            value = jnp.where(wide_lane < 16 * rows, value, 0.0)
            return jnp.concatenate([value, jnp.zeros_like(value)], 1)

        cells[f, pl.ds(0, COLS)] = pltpu.roll(line(both[:, :128], used_rows), shift_own, 1) + pltpu.roll(
            line(both[:, 128:], row_counts[1 - band]), shift_other, 1
        )

    cells[:, pl.ds(COLS, 8)] = jnp.zeros((cells.shape[0], 8, 256), F32)
    def some_cells(i, _):
        for r in range(5):
            frame_cells(5 * i + r)
        return 0

    lax.fori_loop(0, window.shape[0] // 5, some_cells, 0)

    b_in, b_one, b_two = (ref[...].reshape(1, 384) for ref in (b_in, b_one, b_two))
    half_one, half_two = (0.5 * ref[...].reshape(1, 384) for ref in (gain_one, gain_two))
    base_col = column * span

    def inside(shape, axis, shift):
        spot = lax.broadcasted_iota(jnp.int32, shape, axis) + base_col - shift
        return jnp.logical_and(spot >= 0, spot < width)

    zero_row1 = jnp.where(band == 0, 0, used_rows + 2)
    zero_row2 = jnp.where(band == 0, 0, used_rows + 1)

    def in_row(j):
        shift = lax.rem(256 - 16 * j, 256)
        beside = lax.rem(256 + 64 - 16 * j, 256)
        frames = []
        for f in range(cells.shape[0]):
            taps = [
                pltpu.roll(cells[f, pl.ds(1 + d, COLS)], beside if d == 1 else shift, 1)[:, :128]
                for d in range(3)
            ]
            frames.append(
                jnp.concatenate([jnp.where(lane < 64, taps[0], taps[1]), taps[2]], 1).astype(BF16)
            )
        parts = [jnp.concatenate(frames[dt : dt + 8], 0) for dt in range(3)]
        first = jnp.dot(jnp.concatenate(parts, -1), w_in[...], preferred_element_type=F32)
        first = first + b_in
        split = first.reshape(4, 2, COLS, 384)
        for e in range(2):
            first_s[e, j] = split[2:, e].astype(BF16)
        frame = lax.broadcasted_iota(jnp.int32, (8, COLS, 1), 0) + start - 4
        live = jnp.logical_and(inside((8, COLS, 1), 1, 2), frame >= 0)
        act = rms_silu(first.reshape(8, COLS, 384), half_one, live)
        act = act.astype(BF16).reshape(1, 4, 2, COLS, 384)
        store_transformed(v1, pl.ds(j + 1 - band, 1), act[:, :, 0], act[:, :, 1], 3)

    def in_rows(i, _):
        for r in range(2):
            in_row(2 * i + r)
        return 0

    lax.fori_loop(0, (used_rows + 3) // 2, in_rows, 0)
    v1[:, pl.ds(zero_row1, 1)] = jnp.zeros((4, 1, 3, COLS, 384), BF16)

    for copy in copies1:
        copy.wait()
    transform_weight(w1, 0, 128)

    def next_weight(g):
        for copy in height_copies(w2_hbm, w2, sems2, g):
            copy.wait()

    def mid_rows(i, count):
        size = count * 3 * COLS
        shape = (count, 3, COLS, 1)
        frame = 2 * lax.broadcasted_iota(jnp.int32, shape, 1) + start - 2
        column_live = inside(shape, 2, 1)
        for e, value in enumerate(time_conv(v1, w1, i, count)):
            live = jnp.logical_and(column_live, frame + e >= 0)
            acts[e, pl.ds(0, size)] = rms_silu(value + b_one, half_two, live).reshape(size, 384)
        for d in range(3):
            even, odd = (
                acts[e, pl.ds(d, size)].reshape(count, 3, COLS, 384)[:, :, :span].astype(BF16)
                for e in range(2)
            )
            store_transformed(
                v2, pl.ds(i + 1 - band, count), even, odd, 2, pl.ds(d * 384, 384)
            )

    def fours(g, _):
        next_weight(g)
        mid_rows(4 * g, 4)
        transform_rows(w2, g, 1)
        return 0

    def threes(g, _):
        next_weight(n_fours + g)
        mid_rows(4 * n_fours + 3 * g, 3)
        transform_rows(w2, n_fours + g, 1)
        return 0

    def late_weight(g, _):
        next_weight(g)
        transform_rows(w2, g, 1)
        return 0

    n_fours = jnp.where(used_rows == 6, 1, jnp.where(used_rows == 7, 2, 0))
    n_threes = jnp.where(used_rows == 8, 3, jnp.where(used_rows == 7, 0, jnp.where(used_rows == 6, 1, 2)))
    lax.fori_loop(0, n_fours, fours, 0)
    lax.fori_loop(0, n_threes, threes, 0)
    lax.fori_loop(n_fours + n_threes, 3, late_weight, 0)
    v2[:, pl.ds(zero_row2, 1)] = jnp.zeros((4, 1) + v2.shape[2:], BF16)

    def out_rows(count):
        size = count * 2 * span
        sums[...] = jnp.zeros_like(sums)

        def out_part(q, _):
            taps = [v2[q, pl.ds(d, count)].reshape(size, 1152) for d in range(3)]
            value = jnp.dot(
                jnp.concatenate(taps, -1), w2[q].reshape(3456, 384), preferred_element_type=F32
            )
            used = pl.ds(0, size)
            sums[0, used] += jnp.where(q < 3, 1.0, 0.0) * value
            sums[1, used] += jnp.where(q == 0, 0.0, jnp.where(q == 1, 1.0, -1.0)) * value
            return 0

        lax.fori_loop(0, 4, out_part, 0)

    @pl.when(used_rows > 6)
    def _():
        out_rows(8)

    @pl.when(used_rows <= 6)
    def _():
        out_rows(6)

    row = lax.broadcasted_iota(jnp.int32, (8, span, 1), 0)
    for e in range(2):
        first = first_s[e, pl.ds(2 * band, 8)].astype(F32).reshape(16 * COLS, 384)
        first = pltpu.roll(first, 16 * COLS - 2, 0).reshape(8, 2, COLS, 384)[:, :, :span]
        total = sums[e].reshape(8, 2, span, 384) + b_two + first
        for p in range(2):
            live = jnp.logical_and(row < used_rows, 2 * p + e < used_frames)
            out[2 * p + e] = jnp.where(live, total[:, p], 0.0).astype(BF16)


def from_before(value, steps):
    count = lax.axis_size("stretch")
    pairs = [
        (k * 2 + j, (k + steps + j) * 2 + j) for j in range(2) for k in range(count - steps - j)
    ]
    return lax.ppermute(value, ("stretch", "rows"), pairs)


def swapped(value):
    return lax.ppermute(value, "rows", [(0, 1), (1, 0)])


def on_device(
    latent, frame_counts, row_counts, w_in, b_in, gain_one, w_one, b_one, gain_two, w_two, b_two
):
    depth, slots, packed = latent.shape
    span = packed // w_in.shape[3]
    n_cols = lax.axis_size("cols")
    smem = pl.BlockSpec(memory_space=pltpu.SMEM)
    vmem = pl.BlockSpec(memory_space=pltpu.VMEM)
    anywhere = pl.BlockSpec(memory_space=pl.ANY)
    n_window = 6 + depth

    cells = latent.reshape(depth, slots, span, packed // span)
    cells = cells.transpose(0, 2, 1, 3).reshape(depth, span, slots * packed // span)
    cells = jnp.concatenate([cells, swapped(cells)], 2)
    right = [(i, i + 1) for i in range(n_cols - 1)]
    left = [(i + 1, i) for i in range(n_cols - 1)]
    low = lax.ppermute(cells[:, span - 4 :], "cols", right)
    high = lax.ppermute(cells[:, :4], "cols", left)
    wide = jnp.concatenate([low, cells, high], 1)
    held = sum(frame_counts[i : i - 5] for i in range(1, 5))
    wide, short = lax.optimization_barrier((wide, jnp.any(held < 6)))
    near, far = from_before(wide, 1), from_before(wide, 3)
    near_other, far_other = swapped(near), swapped(far)

    def further_back(wide):
        used = frame_counts[lax.axis_index("stretch")]
        last = lax.dynamic_slice_in_dim(jnp.pad(wide, ((2, 0), (0, 0), (0, 0))), used, 2, 0)
        found = from_before(last, 5)
        return jnp.concatenate([found, swapped(found)], 0)

    furthest = lax.cond(short, further_back, lambda wide: jnp.zeros_like(wide), wide)
    return pl.pallas_call(
        functools.partial(kernel, width=span * n_cols, span=span),
        out_shape=jax.ShapeDtypeStruct((depth, slots, span, 384), BF16),
        in_specs=[smem, smem] + [vmem] * 12 + [anywhere] * 2,
        out_specs=vmem,
        scratch_shapes=[
            pltpu.VMEM((4, 1152, 1152), BF16),
            pltpu.VMEM((4, 3, 3, 384, 384), BF16),
            pltpu.VMEM((4, 11, 3, COLS, 384), BF16),
            pltpu.VMEM((4, 10, 2, span, 1152), BF16),
            pltpu.VMEM((2, 10, 2, COLS, 384), BF16),
            pltpu.VMEM((n_window, COLS, 256), BF16),
            pltpu.VMEM((n_window, COLS + 8, 256), F32),
            pltpu.VMEM((768, 384), BF16),
            pltpu.VMEM((2, 12 * COLS + 8, 384), F32),
            pltpu.VMEM((2, 16 * span, 384), F32),
            pltpu.SemaphoreType.DMA((27,)),
            pltpu.SemaphoreType.DMA((9,)),
        ],
        compiler_params=pltpu.CompilerParams(vmem_limit_bytes=57 * 2**20),
        name="block",
    )(
        *(row_counts, frame_counts, wide, near, far, furthest),
        *(near_other, far_other, w_in),
        *(b_in, gain_one, b_one, gain_two, b_two, w_one, w_two),
    )


def solution(mesh):
    placed = (P("stretch", "rows", "cols"), P(), P(), P(), P(), P(), P(), P(), P(), P(), P())
    return jax.shard_map(
        on_device,
        mesh=mesh,
        in_specs=placed,
        out_specs=P("stretch", "rows", "cols", None),
        check_vma=False,
    )
```

```python
import functools

import jax
import jax.numpy as jnp
from jax import lax
from jax.experimental import pallas as pl
from jax.experimental.pallas import tpu as pltpu
from jax.sharding import PartitionSpec as P

F32 = jnp.float32
BF16 = jnp.bfloat16
COLS = 32
SLOT = (0, 1, 3)


def rms_silu(values, half_gain, live):
    inverse = lax.rsqrt(jnp.mean(values * values, axis=-1, keepdims=True) + 1e-06)
    half = values * jnp.where(live, inverse, 0.0) * half_gain
    return half + half * jnp.tanh(half)


def weight_copies(source, target, sems):
    copies = []
    for dt in range(3):
        for dh in range(3):
            for dw in range(3):
                copies.append(
                    pltpu.make_async_copy(
                        source.at[dt, dh, dw],
                        target.at[SLOT[dt], pl.ds(dh * 384, 384), pl.ds(dw * 384, 384)],
                        sems.at[dt * 9 + dh * 3 + dw],
                    )
                )
    return copies


def transform_rows(weight, first, count):
    rows = pl.ds(first, count)
    ends = weight[0, rows] + weight[3, rows]
    middle = weight[1, rows]
    weight[1, rows] = ends + middle
    weight[2, rows] = ends - middle


def transform_weight(weight, start, step):
    def one(i, _):
        transform_rows(weight, pl.multiple_of(i * step, step), step)
        return 0

    lax.fori_loop(start, weight.shape[1] // step, one, 0)


def height_copies(source, target, sems, dh):
    return [
        pltpu.make_async_copy(source.at[dt, dh], target.at[SLOT[dt], dh], sems.at[dt * 3 + dh])
        for dt in range(3)
    ]


def store_transformed(target, rows, even, odd, pairs, lanes=pl.ds(0, 384)):
    here, after = (slice(0, pairs), slice(1, pairs + 1))
    half = jnp.asarray(0.5, BF16)
    target[0, rows, :, :, lanes] = even[:, here] - even[:, after]
    target[1, rows, :, :, lanes] = (odd[:, here] + even[:, after]) * half
    target[2, rows, :, :, lanes] = (even[:, after] - odd[:, here]) * half
    target[3, rows, :, :, lanes] = odd[:, here] - odd[:, after]


def time_conv(field, weight, start, rows):
    pairs = field.shape[2]
    size = rows * pairs * COLS

    def part(q):
        taps = [
            field[q, pl.ds(start + d, rows)].reshape(size, 384) for d in range(3)
        ]
        return jnp.dot(
            jnp.concatenate(taps, -1), weight[q], preferred_element_type=F32
        )

    def joined(wide):
        return (
            wide[:, :384]
            + pltpu.roll(wide[:, 384:768], size - 1, 0)
            + pltpu.roll(wide[:, 768:], size - 2, 0)
        )

    one, two = part(1), part(2)
    even = joined(part(0) + (one + two))
    odd = joined((one - two) - part(3))
    shape = (rows, pairs, COLS, 384)
    return even.reshape(shape), odd.reshape(shape)


def position(frame_counts):
    group = lax.axis_index("stretch")
    last = frame_counts.shape[0] - 1

    def add(k, total):
        return total + jnp.where(k < group, frame_counts[k], 0)

    start = lax.fori_loop(0, last + 1, add, jnp.int32(0))
    before = []
    for s in range(1, 7):
        count = frame_counts[jnp.maximum(group - s, 0)]
        before.append(jnp.where(group >= s, count, 0))
    return frame_counts[group], start, before


def fill_window(window, wide, mine, theirs, start, before, band):
    window[pl.ds(0, 6)] = jnp.zeros((6,) + window.shape[1:], BF16)
    window[pl.ds(6, 4)] = wide[...]

    def halo(w, _):
        frame = start - 6 + w
        end = start
        for d, count in enumerate(before):
            low = end - count
            slot = frame - low if d < 4 else frame - end + 2
            held = jnp.logical_and(jnp.logical_and(frame >= low, frame < end), frame >= 0)
            end = low

            @pl.when(jnp.logical_and(held, band == d % 2))
            def _(slot=slot, source=mine[d // 2]):
                window[pl.ds(w, 1)] = source[pl.ds(slot, 1)]

            @pl.when(jnp.logical_and(held, band != d % 2))
            def _(slot=slot, source=theirs[d // 2]):
                slab = source[pl.ds(slot, 1)]
                window[pl.ds(w, 1)] = jnp.concatenate([slab[:, :, 128:], slab[:, :, :128]], 2)

        return 0

    lax.fori_loop(0, 6, halo, 0)


def kernel(
    row_counts,
    frame_counts,
    wide,
    near,
    far,
    furthest,
    near_other,
    far_other,
    w_in_ref,
    b_in,
    gain_one,
    b_one,
    gain_two,
    b_two,
    w1_hbm,
    w2_hbm,
    out,
    w1,
    w2,
    v1,
    v2,
    first_s,
    window,
    cells,
    w_in,
    acts,
    sums,
    sems,
    sems2,
    *,
    width,
    span,
):
    copies1 = weight_copies(w1_hbm, w1, sems)
    for copy in copies1:
        copy.start()
    band = lax.axis_index("rows")
    column = lax.axis_index("cols")
    used_rows = row_counts[band]
    used_frames, start, before = position(frame_counts)

    w_in[...] = jnp.zeros_like(w_in)
    for dt in range(3):
        for dh in range(3):
            for dw in range(3):
                w_in[pl.ds(dt * 256 + dw * 64 + dh * 16, 16)] = w_in_ref[dt, dh, dw]

    mine = (near, far, furthest)
    theirs = (near_other, far_other, furthest.at[pl.ds(2, 2)])
    fill_window(window, wide, mine, theirs, start, before, band)

    shift_own = jnp.where(band == 0, 16, 48)
    shift_other = jnp.where(band == 0, 16 * (used_rows + 1), 256 - 16 * (row_counts[0] - 3))
    lane = lax.broadcasted_iota(jnp.int32, (COLS, 128), 1)
    wide_lane = lax.broadcasted_iota(jnp.int32, (wide.shape[1], 128), 1)

    def frame_cells(f):
        both = window[f].astype(F32)

        def line(value, rows):
            value = jnp.where(wide_lane < 16 * rows, value, 0.0)
            return jnp.concatenate([value, jnp.zeros_like(value)], 1)

        cells[f, pl.ds(0, COLS)] = pltpu.roll(line(both[:, :128], used_rows), shift_own, 1) + pltpu.roll(
            line(both[:, 128:], row_counts[1 - band]), shift_other, 1
        )

    cells[:, pl.ds(COLS, 8)] = jnp.zeros((cells.shape[0], 8, 256), F32)
    def some_cells(i, _):
        for r in range(5):
            frame_cells(5 * i + r)
        return 0

    lax.fori_loop(0, window.shape[0] // 5, some_cells, 0)

    b_in, b_one, b_two = (ref[...].reshape(1, 384) for ref in (b_in, b_one, b_two))
    half_one, half_two = (0.5 * ref[...].reshape(1, 384) for ref in (gain_one, gain_two))
    base_col = column * span

    def inside(shape, axis, shift):
        spot = lax.broadcasted_iota(jnp.int32, shape, axis) + base_col - shift
        return jnp.logical_and(spot >= 0, spot < width)

    zero_row1 = jnp.where(band == 0, 0, used_rows + 2)
    zero_row2 = jnp.where(band == 0, 0, used_rows + 1)

    def in_row(j):
        shift = lax.rem(256 - 16 * j, 256)
        beside = lax.rem(256 + 64 - 16 * j, 256)
        frames = []
        for f in range(cells.shape[0]):
            taps = [
                pltpu.roll(cells[f, pl.ds(1 + d, COLS)], beside if d == 1 else shift, 1)[:, :128]
                for d in range(3)
            ]
            frames.append(
                jnp.concatenate([jnp.where(lane < 64, taps[0], taps[1]), taps[2]], 1).astype(BF16)
            )
        parts = [jnp.concatenate(frames[dt : dt + 8], 0) for dt in range(3)]
        first = jnp.dot(jnp.concatenate(parts, -1), w_in[...], preferred_element_type=F32)
        first = first + b_in
        split = first.reshape(4, 2, COLS, 384)
        for e in range(2):
            first_s[e, j] = split[2:, e].astype(BF16)
        frame = lax.broadcasted_iota(jnp.int32, (8, COLS, 1), 0) + start - 4
        live = jnp.logical_and(inside((8, COLS, 1), 1, 2), frame >= 0)
        act = rms_silu(first.reshape(8, COLS, 384), half_one, live)
        act = act.astype(BF16).reshape(1, 4, 2, COLS, 384)
        store_transformed(v1, pl.ds(j + 1 - band, 1), act[:, :, 0], act[:, :, 1], 3)

    def in_rows(i, _):
        for r in range(2):
            in_row(2 * i + r)
        return 0

    for dh in range(3):
        for copy in height_copies(w2_hbm, w2, sems2, dh):
            copy.start()
    lax.fori_loop(0, (used_rows + 3) // 2, in_rows, 0)
    v1[:, pl.ds(zero_row1, 1)] = jnp.zeros((4, 1, 3, COLS, 384), BF16)

    for copy in copies1:
        copy.wait()
    transform_weight(w1, 0, 128)

    def next_weight(g):
        for copy in height_copies(w2_hbm, w2, sems2, g):
            copy.wait()

    def mid_rows(i, count):
        size = count * 3 * COLS
        shape = (count, 3, COLS, 1)
        frame = 2 * lax.broadcasted_iota(jnp.int32, shape, 1) + start - 2
        column_live = inside(shape, 2, 1)
        for e, value in enumerate(time_conv(v1, w1, i, count)):
            live = jnp.logical_and(column_live, frame + e >= 0)
            acts[e, pl.ds(0, size)] = rms_silu(value + b_one, half_two, live).reshape(size, 384)
        for d in range(3):
            even, odd = (
                acts[e, pl.ds(d, size)].reshape(count, 3, COLS, 384)[:, :, :span].astype(BF16)
                for e in range(2)
            )
            store_transformed(
                v2, pl.ds(i + 1 - band, count), even, odd, 2, pl.ds(d * 384, 384)
            )

    def fours(g, _):
        mid_rows(4 * g, 4)
        next_weight(g)
        transform_rows(w2, g, 1)
        return 0

    def threes(g, _):
        mid_rows(4 * n_fours + 3 * g, 3)
        next_weight(n_fours + g)
        transform_rows(w2, n_fours + g, 1)
        return 0

    def late_weight(g, _):
        next_weight(g)
        transform_rows(w2, g, 1)
        return 0

    n_fours = jnp.where(used_rows == 6, 1, jnp.where(used_rows == 7, 2, 0))
    n_threes = jnp.where(used_rows == 8, 3, jnp.where(used_rows == 7, 0, jnp.where(used_rows == 6, 1, 2)))
    lax.fori_loop(0, n_fours, fours, 0)
    lax.fori_loop(0, n_threes, threes, 0)
    lax.fori_loop(n_fours + n_threes, 3, late_weight, 0)
    v2[:, pl.ds(zero_row2, 1)] = jnp.zeros((4, 1) + v2.shape[2:], BF16)

    def out_rows(count):
        size = count * 2 * span
        sums[...] = jnp.zeros_like(sums)

        def out_part(q, _):
            taps = [v2[q, pl.ds(d, count)].reshape(size, 1152) for d in range(3)]
            value = jnp.dot(
                jnp.concatenate(taps, -1), w2[q].reshape(3456, 384), preferred_element_type=F32
            )
            used = pl.ds(0, size)
            sums[0, used] += jnp.where(q < 3, 1.0, 0.0) * value
            sums[1, used] += jnp.where(q == 0, 0.0, jnp.where(q == 1, 1.0, -1.0)) * value
            return 0

        lax.fori_loop(0, 4, out_part, 0)

    @pl.when(used_rows > 6)
    def _():
        out_rows(8)

    @pl.when(used_rows <= 6)
    def _():
        out_rows(6)

    row = lax.broadcasted_iota(jnp.int32, (8, span, 1), 0)
    for e in range(2):
        first = first_s[e, pl.ds(2 * band, 8)].astype(F32).reshape(16 * COLS, 384)
        first = pltpu.roll(first, 16 * COLS - 2, 0).reshape(8, 2, COLS, 384)[:, :, :span]
        total = sums[e].reshape(8, 2, span, 384) + b_two + first
        for p in range(2):
            live = jnp.logical_and(row < used_rows, 2 * p + e < used_frames)
            out[2 * p + e] = jnp.where(live, total[:, p], 0.0).astype(BF16)


def from_before(value, steps):
    count = lax.axis_size("stretch")
    pairs = [
        (k * 2 + j, (k + steps + j) * 2 + j) for j in range(2) for k in range(count - steps - j)
    ]
    return lax.ppermute(value, ("stretch", "rows"), pairs)


def swapped(value):
    return lax.ppermute(value, "rows", [(0, 1), (1, 0)])


def on_device(
    latent, frame_counts, row_counts, w_in, b_in, gain_one, w_one, b_one, gain_two, w_two, b_two
):
    depth, slots, packed = latent.shape
    span = packed // w_in.shape[3]
    n_cols = lax.axis_size("cols")
    smem = pl.BlockSpec(memory_space=pltpu.SMEM)
    vmem = pl.BlockSpec(memory_space=pltpu.VMEM)
    anywhere = pl.BlockSpec(memory_space=pl.ANY)
    n_window = 6 + depth

    cells = latent.reshape(depth, slots, span, packed // span)
    cells = cells.transpose(0, 2, 1, 3).reshape(depth, span, slots * packed // span)
    cells = jnp.concatenate([cells, swapped(cells)], 2)
    right = [(i, i + 1) for i in range(n_cols - 1)]
    left = [(i + 1, i) for i in range(n_cols - 1)]
    low = lax.ppermute(cells[:, span - 4 :], "cols", right)
    high = lax.ppermute(cells[:, :4], "cols", left)
    wide = jnp.concatenate([low, cells, high], 1)
    held = sum(frame_counts[i : i - 5] for i in range(1, 5))
    wide, short = lax.optimization_barrier((wide, jnp.any(held < 6)))
    near, far = from_before(wide, 1), from_before(wide, 3)
    near_other, far_other = swapped(near), swapped(far)

    def further_back(wide):
        used = frame_counts[lax.axis_index("stretch")]
        last = lax.dynamic_slice_in_dim(jnp.pad(wide, ((2, 0), (0, 0), (0, 0))), used, 2, 0)
        found = from_before(last, 5)
        return jnp.concatenate([found, swapped(found)], 0)

    furthest = lax.cond(short, further_back, lambda wide: jnp.zeros_like(wide), wide)
    return pl.pallas_call(
        functools.partial(kernel, width=span * n_cols, span=span),
        out_shape=jax.ShapeDtypeStruct((depth, slots, span, 384), BF16),
        in_specs=[smem, smem] + [vmem] * 12 + [anywhere] * 2,
        out_specs=vmem,
        scratch_shapes=[
            pltpu.VMEM((4, 1152, 1152), BF16),
            pltpu.VMEM((4, 3, 3, 384, 384), BF16),
            pltpu.VMEM((4, 11, 3, COLS, 384), BF16),
            pltpu.VMEM((4, 10, 2, span, 1152), BF16),
            pltpu.VMEM((2, 10, 2, COLS, 384), BF16),
            pltpu.VMEM((n_window, COLS, 256), BF16),
            pltpu.VMEM((n_window, COLS + 8, 256), F32),
            pltpu.VMEM((768, 384), BF16),
            pltpu.VMEM((2, 12 * COLS + 8, 384), F32),
            pltpu.VMEM((2, 16 * span, 384), F32),
            pltpu.SemaphoreType.DMA((27,)),
            pltpu.SemaphoreType.DMA((9,)),
        ],
        compiler_params=pltpu.CompilerParams(vmem_limit_bytes=57 * 2**20),
        name="block",
    )(
        *(row_counts, frame_counts, wide, near, far, furthest),
        *(near_other, far_other, w_in),
        *(b_in, gain_one, b_one, gain_two, b_two, w_one, w_two),
    )


def solution(mesh):
    placed = (P("stretch", "rows", "cols"), P(), P(), P(), P(), P(), P(), P(), P(), P(), P())
    return jax.shard_map(
        on_device,
        mesh=mesh,
        in_specs=placed,
        out_specs=P("stretch", "rows", "cols", None),
        check_vma=False,
    )
```
